256 devices in a mesh: ctx: 16 (over z_lo, y), tp: 8 (over x, core), pd: 2 (over z_hi).
Axes of the slice: x: 4, y: 4, z: 8 (z_hi: 2, z_lo: 4; z = z_hi * 4 + z_lo), core: 2. Of those that a mesh axis runs over, the one named last changes fastest.
Arguments:
- prefill_query: bfloat16 [2, 2, 4096, 8192], P('pd', None, 'ctx', 'tp'), may hold values from -24 to 24
- prefill_kv: bfloat16 [2, 2, 4096, 2048], P('pd', None, 'ctx', 'tp'), may hold values from -8 to 8
- decode_query: bfloat16 [2, 16, 16, 4, 8192], P('pd', 'ctx', None, None, 'tp'), may hold values from -24 to 24
- gen_cache: bfloat16 [2, 16, 16, 256, 2048], P('pd', 'ctx', None, None, 'tp'), may hold values from -8 to 8
- new_hidden: bfloat16 [2, 16, 16, 4, 8192], P('pd', 'ctx', None, None, 'tp'), may hold values from -6 to 6
- norm_gain: float32 [8192], replicated, may hold values from 0.1 to 1.9
- kv_weight: bfloat16 [8192, 2048], P(None, 'tp'), may hold values from -0.125 to 0.125
- prompt_of: int32 [2, 16], replicated, may hold values from 0 to 1, as said below
- cached_len: int32 [2, 16, 16], P('pd', 'ctx'), may hold values from 64 to 256, as said below
Outputs:
- segment_attention: bfloat16 [2, 2, 4096, 8192], P('pd', None, 'ctx', 'tp')
- decode_attention: bfloat16 [2, 16, 16, 4, 8192], P('pd', 'ctx', None, None, 'tp')
The draws below stay inside these ranges and needn't reach their ends.
Inputs may be any that keep to these rules, and one draw needn't show every extreme that they name: `prompt_of`: in each pool every prompt is named by exactly 8 replicas. `cached_len`: in every pool and replica some completion holds exactly 256 slots and another exactly 64.
All inputs are finite; a program needn't handle non-finite values.
Results may differ from the reference program's by a relative error of at most 0.005.
Values may be sent and summed in bfloat16 or wider, within the bound.
No kernel may reach another device: no remote copies, remote signals or barrier semaphores. Data moves between devices by JAX's collectives and lax.ppermute only.
A program may use at most 192 MiB of HBM per device.

```python
import jax
import jax.numpy as jnp
from jax import lax

D = 8192
HD = 128
KVH = 8
GROUP = 8
PROMPTS = 2
SAMPLES = 16
GEN_MAX = 256
STEPS = 4
QH = 64
REPLICAS = 16
SEGMENT = 4096


def normal_uniform(key, shape, spread, width):
    first_key, second_key = jax.random.split(key)
    return spread * jax.random.truncated_normal(first_key, -4.0, 4.0, shape) + jax.random.uniform(second_key, shape, minval=-width, maxval=width)


def draw_prefill_kv(key, part):
    shape_rows = (2, PROMPTS, SEGMENT, KVH, HD)
    key_rows = normal_uniform(key, shape_rows, 2.0, 0.0)
    key = jax.random.fold_in(key, 1)
    val_rows = jax.random.truncated_normal(key, -6.0, 6.0, shape_rows)
    return jnp.stack([key_rows, val_rows], axis=-2).reshape(2, PROMPTS, SEGMENT, KVH * 2 * HD).astype(jnp.bfloat16)


def draw_prefill_query(key, part):
    key = jax.random.fold_in(key, 2)
    shape_query = (2, PROMPTS, SEGMENT, KVH, GROUP, HD)
    queries = jax.random.truncated_normal(key, -6.0, 6.0, shape_query)
    return queries.reshape(2, PROMPTS, SEGMENT, KVH * GROUP * HD).astype(jnp.bfloat16)


def draw_gen_cache(key, part):
    shape_rows = (2, REPLICAS, SAMPLES, GEN_MAX, KVH, HD)
    key_rows = normal_uniform(key, shape_rows, 2.0, 0.0)
    key = jax.random.fold_in(key, 3)
    val_rows = jax.random.truncated_normal(key, -6.0, 6.0, shape_rows)
    return jnp.stack([key_rows, val_rows], axis=-2).reshape(2, REPLICAS, SAMPLES, GEN_MAX, KVH * 2 * HD).astype(jnp.bfloat16)


def draw_decode_query(key, part):
    key = jax.random.fold_in(key, 4)
    shape_query = (2, REPLICAS, SAMPLES, STEPS, KVH, GROUP, HD)
    queries = jax.random.truncated_normal(key, -6.0, 6.0, shape_query)
    return queries.reshape(2, REPLICAS, SAMPLES, STEPS, KVH * GROUP * HD).astype(jnp.bfloat16)


def draw_cached_len(key, part):
    key = jax.random.fold_in(key, 5)
    lengths = jax.random.randint(key, (2, REPLICAS, SAMPLES), GEN_MAX // 4, GEN_MAX + 1)
    longest = jax.random.randint(jax.random.fold_in(key, 1), (2, REPLICAS, 1), 0, SAMPLES)
    shortest = (longest + 1) % SAMPLES
    sample_index = jnp.arange(SAMPLES)[None, None, :]
    lengths = jnp.where(sample_index == longest, GEN_MAX, lengths)
    lengths = jnp.where(sample_index == shortest, GEN_MAX // 4, lengths)
    return lengths.astype(jnp.int32)


def draw_prompt_of(key, part):
    key = jax.random.fold_in(key, 6)
    first = jax.random.permutation(jax.random.fold_in(key, 1), REPLICAS)
    second = jax.random.permutation(jax.random.fold_in(key, 2), REPLICAS)
    return (jnp.stack([first, second]) % PROMPTS).astype(jnp.int32)


def block_levels(rng, shape, pieces, least, largest):
    gain = 1.0
    for dim, blocks in pieces:
        draws = jax.random.uniform(jax.random.fold_in(jax.random.fold_in(rng, 6), dim), (blocks,), jnp.float32, least / len(pieces), largest / len(pieces))
        gain = gain * jnp.repeat(jnp.exp(draws), shape[dim] // blocks).reshape((-1,) + (1,) * (len(shape) - 1 - dim))
    return gain


def normal_values(key, shape, deviation, bound, cuts=(), kind=jnp.bfloat16):
    result = deviation * jax.random.normal(key, shape, jnp.float32)
    if cuts:
        result = result * block_levels(key, shape, cuts, -0.22, 0.18)
    return jnp.clip(result, -bound, bound).astype(kind)


def setup_inputs(seed: int = 0) -> dict:
    keys = jax.random.split(jax.random.key(seed), 10)
    return {
        "prefill_query": draw_prefill_query(jax.random.fold_in(keys[9], 71), 0),
        "prefill_kv": draw_prefill_kv(jax.random.fold_in(keys[9], 71), 0),
        "decode_query": draw_decode_query(jax.random.fold_in(keys[9], 71), 0),
        "gen_cache": draw_gen_cache(jax.random.fold_in(keys[9], 71), 0),
        "new_hidden": normal_values(keys[4], (2, REPLICAS, SAMPLES, STEPS, D), 1.0, 6.0, ((0, 2), (1, 16), (4, 8))),
        "norm_gain": jnp.clip(1.0 + 0.18 * jax.random.normal(keys[5], (D,), jnp.float32), 0.1, 1.9),
        "kv_weight": normal_values(keys[6], (D, KVH * 2 * HD), (D // 4) ** -0.5, 0.125, ((1, 8),)),
        "prompt_of": draw_prompt_of(jax.random.fold_in(keys[9], 71), 0),
        "cached_len": draw_cached_len(jax.random.fold_in(keys[9], 71), 0),
    }


masked_score = -1e+30

def rotate_keys(key_rows, positions):
    half_dim = HD // 2
    frequency = 1000000.0 ** (-jnp.arange(half_dim, dtype=jnp.float32) * 2.0 / HD)
    angles = positions[..., None] * frequency
    first_half = key_rows[..., :half_dim]
    second_half = key_rows[..., half_dim:]
    cosine = jnp.cos(angles)
    sine_part = jnp.sin(angles)
    return jnp.concatenate([first_half * cosine - second_half * sine_part, second_half * cosine + first_half * sine_part], axis=-1)

def barrier_round(weights):
    return lax.optimization_barrier(weights.astype(jnp.bfloat16)).astype(jnp.float32)

def reference(prefill_query, prefill_kv, decode_query, gen_cache, new_hidden, norm_gain, kv_weight, prompt_of, cached_len):
    score_scale = HD ** (-0.5)
    query_items = prefill_query.reshape(2 * PROMPTS, SEGMENT, KVH, GROUP, HD)
    kv_items = prefill_kv.reshape(2 * PROMPTS, SEGMENT, KVH, 2, HD)
    positions = jnp.arange(SEGMENT, dtype=jnp.int32)
    causal = positions[None, :] <= positions[:, None]

    def prefill_prompt(prompt_item):
        queries, keyvals = prompt_item
        scores = jnp.einsum('ckgd,jkd->kgcj', queries.astype(jnp.float32), keyvals[:, :, 0].astype(jnp.float32)) * score_scale
        scores = jnp.where(causal, scores, masked_score)
        highest = lax.optimization_barrier(jnp.max(scores, axis=-1, keepdims=True))
        weights = jnp.where(causal, jnp.exp(scores - highest), 0.0)
        totals = lax.optimization_barrier(jnp.sum(weights, axis=-1))
        mixed = jnp.einsum('kgcj,jkd->kgcd', barrier_round(weights), keyvals[:, :, 1].astype(jnp.float32)) / totals[..., None]
        return jnp.transpose(mixed, (2, 0, 1, 3)).reshape(SEGMENT, QH * HD).astype(jnp.bfloat16)
    segment_attention = lax.map(prefill_prompt, (query_items, kv_items)).reshape(2, PROMPTS, SEGMENT, QH * HD)
    kv_pools = prefill_kv.reshape(2, PROMPTS, SEGMENT, KVH, 2, HD)
    relayed = jnp.stack([jnp.take(kv_pools[1 - pool_index], prompt_of[1 - pool_index].astype(jnp.int32), axis=0) for pool_index in range(2)])
    hidden = new_hidden.astype(jnp.float32)
    scaled = (hidden * norm_gain).astype(jnp.bfloat16)
    projected = jnp.dot(scaled.reshape(-1, D), kv_weight, preferred_element_type=jnp.float32).reshape(2, REPLICAS, SAMPLES, STEPS, KVH * 2 * HD)
    inverse_rms = lax.rsqrt(lax.optimization_barrier(jnp.mean(hidden * hidden, axis=-1)) + 1e-06)
    normed = (projected * inverse_rms[..., None]).reshape(2, REPLICAS, SAMPLES, STEPS, KVH, 2, HD)
    new_positions = (SEGMENT + cached_len[..., None] + jnp.arange(STEPS, dtype=jnp.int32)).astype(jnp.float32)
    rotated = rotate_keys(normed[..., 0, :], new_positions[..., None])
    fresh_kv = jnp.stack([rotated, normed[..., 1, :]], axis=-2).astype(jnp.bfloat16)
    slot_index = jnp.arange(GEN_MAX, dtype=jnp.int32)
    step_index = jnp.arange(STEPS, dtype=jnp.int32)
    fresh_allowed = (step_index[None, :] <= step_index[:, None])[None, :, None, None, :]

    def decode_rows(row_item):
        queries, segment_kv, cache_kv, new_kv, lengths = row_item
        query_wide = queries.astype(jnp.float32)
        segment_scores = jnp.einsum('sqkgd,ckd->sqkgc', query_wide, segment_kv[:, :, 0].astype(jnp.float32)) * score_scale
        cache_scores = jnp.einsum('sqkgd,sjkd->sqkgj', query_wide, cache_kv[:, :, :, 0].astype(jnp.float32)) * score_scale
        fresh_scores = jnp.einsum('sqkgd,stkd->sqkgt', query_wide, new_kv[:, :, :, 0].astype(jnp.float32)) * score_scale
        cache_allowed = (slot_index[None, :] < lengths[:, None])[:, None, None, None, :]
        cache_scores = jnp.where(cache_allowed, cache_scores, masked_score)
        fresh_scores = jnp.where(fresh_allowed, fresh_scores, masked_score)
        highest = jnp.maximum(jnp.maximum(lax.optimization_barrier(jnp.max(segment_scores, axis=-1)), lax.optimization_barrier(jnp.max(cache_scores, axis=-1))), lax.optimization_barrier(jnp.max(fresh_scores, axis=-1)))[..., None]
        segment_weights = jnp.exp(segment_scores - highest)
        cache_weights = jnp.where(cache_allowed, jnp.exp(cache_scores - highest), 0.0)
        fresh_weights = jnp.where(fresh_allowed, jnp.exp(fresh_scores - highest), 0.0)
        totals = lax.optimization_barrier(jnp.sum(segment_weights, axis=-1)) + lax.optimization_barrier(jnp.sum(cache_weights, axis=-1)) + lax.optimization_barrier(jnp.sum(fresh_weights, axis=-1))
        mixed = jnp.einsum('sqkgc,ckd->sqkgd', barrier_round(segment_weights), segment_kv[:, :, 1].astype(jnp.float32))
        mixed = mixed + jnp.einsum('sqkgj,sjkd->sqkgd', barrier_round(cache_weights), cache_kv[:, :, :, 1].astype(jnp.float32))
        mixed = mixed + jnp.einsum('sqkgt,stkd->sqkgd', barrier_round(fresh_weights), new_kv[:, :, :, 1].astype(jnp.float32))
        return (mixed / totals[..., None]).reshape(SAMPLES, STEPS, QH * HD).astype(jnp.bfloat16)
    row_items = (decode_query.reshape(2 * REPLICAS, SAMPLES, STEPS, KVH, GROUP, HD), relayed.reshape(2 * REPLICAS, SEGMENT, KVH, 2, HD), gen_cache.reshape(2 * REPLICAS, SAMPLES, GEN_MAX, KVH, 2, HD), fresh_kv.reshape(2 * REPLICAS, SAMPLES, STEPS, KVH, 2, HD), cached_len.reshape(2 * REPLICAS, SAMPLES))
    decode_attention = lax.map(decode_rows, row_items).reshape(2, REPLICAS, SAMPLES, STEPS, QH * HD)
    return (segment_attention, decode_attention)
```

```python
import functools

import jax
import jax.numpy as jnp
from jax import lax
from jax.experimental import pallas as pl
from jax.experimental.pallas import tpu as pltpu
from jax.sharding import PartitionSpec as P

D = 8192
HD = 128
GROUP = 8
BLOCK = 256
MASKED = -1e30
LOG2E = 1.4426950408889634
SCALE2 = HD ** (-0.5) * LOG2E
VMEM_LIMIT = 40 * 1024 * 1024

bf16 = jnp.bfloat16
f32 = jnp.float32


def scores_of(rows, keys):
    return lax.dot_general(rows, keys, (((1,), (1,)), ((), ())), preferred_element_type=f32)


def fill_values(aug_ref, index, block):
    aug_ref[index, :, :HD] = block[:, HD:]
    aug_ref[index, :, HD:] = jnp.ones((BLOCK, HD), bf16)


def weigh(parts, highest, aug_blocks):
    out = None
    for part, aug in zip(parts, aug_blocks):
        weights = jnp.exp2((part - highest) * SCALE2).astype(bf16)
        term = jnp.dot(weights, aug, preferred_element_type=f32)
        out = term if out is None else out + term
    return out


def max_of(parts):
    top = parts[0]
    for part in parts[1:]:
        top = jnp.maximum(top, part)
    return jnp.max(top, axis=-1, keepdims=True)


def first_kernel(info, own_q, partner_q, *refs):
    blocks = refs[:8]
    acc_ref, stat_ref, q_scr, key_scr, aug_scr = refs[8:]
    parity, row_y = info[0], info[1]
    q_scr[0] = own_q[...]
    q_scr[1] = partner_q[...]
    for group in range(2):
        for b in range(4):
            block = blocks[group * 4 + b][...]
            key_scr[group * 4 + b] = block[:, :HD]
            fill_values(aug_scr, group * 4 + b, block)
    lane = lax.broadcasted_iota(jnp.int32, (BLOCK, HD), 1)
    upper = lax.broadcasted_iota(jnp.int32, (BLOCK, BLOCK), 1) > lax.broadcasted_iota(
        jnp.int32, (BLOCK, BLOCK), 0
    )

    def shift_of(b):
        block_y = (row_y + (0, 3, 1, 2)[b]) % 4
        return jnp.where(block_y < row_y, 0.0, MASKED).astype(f32)

    for odd in (True, False):
        side = 1 - parity if odd else parity
        same = side * 4
        other = (1 - side) * 4

        def head(h, carry):
            rows = q_scr[side, :, pl.ds(pl.multiple_of(h * HD, HD), HD)]
            parts = []
            augs = []
            for b in range(4):
                part = scores_of(rows, key_scr[same + b])
                if b == 0:
                    part = jnp.where(upper, MASKED, part)
                else:
                    part = part + shift_of(b)
                parts.append(part)
                augs.append(aug_scr[same + b])
            if odd:
                for b in range(4):
                    parts.append(scores_of(rows, key_scr[other + b]))
                    augs.append(aug_scr[other + b])
            highest = max_of(parts)
            mixed = weigh(parts, highest, augs)
            acc_ref[side, h] = mixed[:, :HD]
            old = jnp.where(lane == h, highest, stat_ref[side])
            stat_ref[side] = jnp.where(lane == h + 8, mixed[:, HD:], old)
            return carry

        lax.fori_loop(0, GROUP, head, 0)


def last_kernel(info, q_ref, acc_ref, stat_ref, *refs):
    kv_refs = refs[:4]
    out_ref, aug_scr = refs[4:]
    lane = lax.broadcasted_iota(jnp.int32, (BLOCK, HD), 1)

    def column(h):
        return jnp.sum(jnp.where(lane == h, stat_ref[0], 0.0), axis=-1, keepdims=True)

    @pl.when(info[2] >= 2)
    def _():
        for b in range(8):
            fill_values(aug_scr, b, kv_refs[b // 2][b % 2])

        def head(h, carry):
            at = pl.ds(pl.multiple_of(h * HD, HD), HD)
            rows = q_ref[:, at]
            parts = [scores_of(rows, kv_refs[b // 2][b % 2, :, :HD]) for b in range(8)]
            before = column(h)
            highest = jnp.maximum(before, max_of(parts))
            mixed = weigh(parts, highest, [aug_scr[b] for b in range(8)])
            fade = jnp.exp2((before - highest) * SCALE2)
            total = column(h + 8) * fade + mixed[:, HD:]
            out_ref[:, at] = ((acc_ref[0, h] * fade + mixed[:, :HD]) / total).astype(bf16)
            return carry

        lax.fori_loop(0, GROUP, head, 0)

    @pl.when(info[2] < 2)
    def _():
        def head(h, carry):
            at = pl.ds(pl.multiple_of(h * HD, HD), HD)
            out_ref[:, at] = (acc_ref[0, h] / column(h + 8)).astype(bf16)
            return carry

        lax.fori_loop(0, GROUP, head, 0)


def segment_kernel(info, q0_ref, q1_ref, *refs):
    near = refs[:8]
    far = refs[8:12]
    out0_ref, out1_ref, aug_scr = refs[12:]

    def keys(b):
        if b < 8:
            return near[b][:, :HD]
        return far[(b - 8) // 2][(b - 8) % 2, :, :HD]

    for b in range(16):
        block = near[b][...] if b < 8 else far[(b - 8) // 2][(b - 8) % 2]
        fill_values(aug_scr, b, block)
    for which, (q_ref, out_ref) in enumerate(((q0_ref, out0_ref), (q1_ref, out1_ref))):

        @pl.when(info[3 + which] == 1)
        def _():
            pieces = []
            for tile in range(2):
                rows = q_ref[tile * 256 : tile * 256 + 256]
                parts = [scores_of(rows, keys(b)) for b in range(16)]
                highest = max_of(parts)
                mixed = weigh(parts, highest, [aug_scr[b] for b in range(16)])
                total = mixed[:, HD:]
                out_ref[tile * 256 : tile * 256 + 256] = (mixed[:, :HD] / total).astype(bf16)
                level = highest * SCALE2 + jnp.log2(total)
                turned = jnp.transpose(level)[0:1]
                pieces += [turned[:, :128], turned[:, 128:]]
            level = jnp.concatenate(pieces, axis=0)
            high = level.astype(bf16)
            rest = level - high.astype(f32)
            middle = rest.astype(bf16)
            low = (rest - middle.astype(f32)).astype(bf16)
            out_ref[512:528] = jnp.concatenate(
                [high.astype(f32), middle.astype(f32), low.astype(f32), jnp.zeros((4, HD), f32)],
                axis=0,
            ).astype(bf16)

        @pl.when(info[3 + which] != 1)
        def _():
            out_ref[...] = jnp.zeros_like(out_ref)


def local_kernel(
    len_ref, hidden_ref, gain_ref, weight_ref, cos_ref, sin_ref, q_ref, cache_ref, out_ref, level_ref
):
    width = hidden_ref.shape[2]
    squares = jnp.zeros((64, 1), f32)
    projected = jnp.zeros((64, 2 * HD), f32)
    for part in range(D // width):
        wide = hidden_ref[part].astype(f32)
        squares = squares + jnp.sum(wide * wide, axis=-1, keepdims=True)
        scaled = (wide * gain_ref[:, part * width : (part + 1) * width]).astype(bf16)
        projected = projected + jnp.dot(
            scaled, weight_ref[part * width : (part + 1) * width], preferred_element_type=f32
        )
    normed = projected * lax.rsqrt(squares / D + 1e-6)
    key_rows = normed[:, :HD]
    turned = jnp.concatenate([key_rows[:, HD // 2 :], key_rows[:, : HD // 2]], axis=1)
    fresh_k = (key_rows * cos_ref[...] + turned * sin_ref[...]).astype(bf16)
    fresh_v = normed[:, HD:].astype(bf16)
    fresh_aug = jnp.concatenate([fresh_v, jnp.ones((64, HD), bf16)], axis=1)
    ones = jnp.ones((BLOCK, HD), bf16)
    slot = lax.broadcasted_iota(jnp.int32, (32, BLOCK), 1)
    fresh_slot = lax.broadcasted_iota(jnp.int32, (32, 64), 1)
    step = lax.broadcasted_iota(jnp.int32, (32, 64), 0) // GROUP

    for s in range(16):
        rows = q_ref[s * 32 : (s + 1) * 32]
        cache_part = jnp.where(
            slot < len_ref[s], scores_of(rows, cache_ref[s, :, :HD]), MASKED
        )
        allowed = (fresh_slot >= s * 4) & (fresh_slot <= s * 4 + step)
        fresh_part = jnp.where(allowed, scores_of(rows, fresh_k), MASKED)
        highest = jnp.maximum(
            jnp.max(cache_part, axis=-1, keepdims=True), jnp.max(fresh_part, axis=-1, keepdims=True)
        )
        cache_aug = jnp.concatenate([cache_ref[s, :, HD:], ones], axis=1)
        mixed = weigh([cache_part, fresh_part], highest, [cache_aug, fresh_aug])
        total = mixed[:, HD:]
        out_ref[s * 32 : (s + 1) * 32] = mixed[:, :HD] / total
        level_ref[s * 32 : (s + 1) * 32] = highest * SCALE2 + jnp.log2(total)


def merge_kernel(info, local_ref, level_ref, same_ref, other_ref, out_ref):
    def merge(part_ref):
        stat = part_ref[512:528].astype(f32)
        level = stat[0:4] + stat[4:8] + stat[8:12]
        for tile in range(4):
            at = slice(tile * 128, tile * 128 + 128)
            far = jnp.transpose(jnp.broadcast_to(level[tile : tile + 1], (128, 128)))
            near = level_ref[at]
            top = jnp.maximum(far, near)
            far_share = jnp.exp2(far - top)
            near_share = jnp.exp2(near - top)
            mixed = part_ref[at].astype(f32) * far_share + local_ref[at] * near_share
            out_ref[at] = (mixed / (far_share + near_share)).astype(bf16)

    @pl.when(info[5] == 1)
    def _():
        merge(same_ref)

    @pl.when(info[5] != 1)
    def _():
        merge(other_ref)


SMEM = pl.BlockSpec(memory_space=pltpu.SMEM)
VMEM = pl.BlockSpec(memory_space=pltpu.VMEM)


def call(kernel, out_shape, args, scalars=1, scratch=(), flops=0, touched=0, exps=0, specs=None):
    in_specs = [SMEM] * scalars + [VMEM] * (len(args) - scalars)
    for place, spec in (specs or {}).items():
        in_specs[place] = spec
    return pl.pallas_call(
        kernel,
        grid=(1,) if specs else (),
        out_shape=out_shape,
        in_specs=in_specs,
        out_specs=jax.tree.map(lambda _: VMEM, out_shape),
        scratch_shapes=list(scratch),
        compiler_params=pltpu.CompilerParams(vmem_limit_bytes=VMEM_LIMIT),
        cost_estimate=pl.CostEstimate(flops=flops, bytes_accessed=touched, transcendentals=exps),
    )(*args)


def y_turn(block, distance):
    route = [(i, i // 4 * 4 + (i % 4 + distance) % 4) for i in range(16)]
    return lax.ppermute(block, "ctx", route)


def z_swap(block, bits):
    return lax.ppermute(block, "ctx", [(i, i ^ (4 * bits)) for i in range(16)])


def y_all(block):
    return [block, y_turn(block, 1), y_turn(block, -1), y_turn(block, 2)]


def pool_swap(block, z_bits):
    route = [(i, (i ^ 1) ^ (8 * z_bits)) for i in range(32)]
    return lax.ppermute(block, ("ctx", "pd"), route)


def on_device(
    prefill_query,
    prefill_kv,
    decode_query,
    gen_cache,
    new_hidden,
    norm_gain,
    kv_weight,
    prompt_of,
    cached_len,
):
    queries = prefill_query[0]
    keyvals = prefill_kv[0]
    place = lax.axis_index("ctx")
    pool = lax.axis_index("pd")
    z, y = place // 4, place % 4
    parity = z % 2
    here = lax.dynamic_index_in_dim(prompt_of, pool, 0, keepdims=False)
    there = lax.dynamic_index_in_dim(prompt_of, 1 - pool, 0, keepdims=False)
    info = jnp.stack(
        [
            parity,
            y,
            z,
            (here[place] == parity).astype(jnp.int32),
            (here[place ^ 4] == parity).astype(jnp.int32),
            (there[place] == parity).astype(jnp.int32),
        ]
    ).astype(jnp.int32)

    even = parity == 0
    kv_keep = jnp.where(even, keyvals[0], keyvals[1])
    kv_give = jnp.where(even, keyvals[1], keyvals[0])
    from_z1 = z_swap(kv_give, 1)
    from_z2 = z_swap(kv_keep, 2)
    from_z3 = z_swap(kv_give, 3)
    group0 = y_all(kv_keep)
    q_keep = jnp.where(even, queries[0], queries[1])
    q_give = jnp.where(even, queries[1], queries[0])
    q_partner = z_swap(q_give, 1)
    group1 = y_all(from_z1)
    group23 = y_all(jnp.stack([from_z2, from_z3]))

    hidden = new_hidden[0, 0]
    samples, steps, width = hidden.shape
    wide = lax.all_gather(hidden.reshape(samples * steps, width), "tp", axis=0)
    step_rows = decode_query[0, 0].reshape(samples * steps * GROUP, HD)
    rows0 = pool_swap(step_rows, 0)
    rows1 = pool_swap(step_rows, 1)

    lengths = cached_len[0, 0]
    half = HD // 2
    frequency = 1000000.0 ** (-jnp.arange(half, dtype=f32) * 2.0 / HD)
    positions = (4096 + lengths[:, None] + jnp.arange(steps, dtype=jnp.int32)[None, :]).astype(f32)
    angles = positions.reshape(-1)[:, None] * frequency
    cosine, sine = jnp.cos(angles), jnp.sin(angles)
    cos_all = jnp.concatenate([cosine, cosine], axis=-1)
    sin_all = jnp.concatenate([-sine, sine], axis=-1)

    shape = jax.ShapeDtypeStruct
    rows = samples * steps * GROUP
    local_out, local_level = call(
        local_kernel,
        (shape((rows, HD), f32), shape((rows, HD), f32)),
        (
            lengths,
            wide,
            norm_gain[None],
            kv_weight,
            cos_all,
            sin_all,
            step_rows,
            gen_cache[0, 0],
        ),
        flops=2 * 64 * D * 256,
        touched=8 << 20,
        exps=rows * 320,
    )

    acc, stat = call(
        first_kernel,
        (shape((2, GROUP, BLOCK, HD), f32), shape((2, BLOCK, HD), f32)),
        (info, q_keep, q_partner, *group0, *group1),
        scratch=(
            pltpu.VMEM((2, BLOCK, GROUP * HD), bf16),
            pltpu.VMEM((8, BLOCK, HD), bf16),
            pltpu.VMEM((8, BLOCK, 2 * HD), bf16),
        ),
        flops=3 * 2048 * 1024 * 512,
        touched=4 << 20,
        exps=3 * 2048 * 1024,
    )
    segment0, segment1 = call(
        segment_kernel,
        (shape((rows + 16, HD), bf16), shape((rows + 16, HD), bf16)),
        (info, rows0, rows1, *group0, *group1, *group23),
        scratch=(pltpu.VMEM((16, BLOCK, 2 * HD), bf16),),
        flops=1024 * 4096 * 512,
        touched=3 << 20,
        exps=1024 * 4096,
    )
    back0 = pool_swap(segment0, 0)
    back1 = pool_swap(segment1, 1)

    def finish(q_rows, side):
        return call(
            last_kernel,
            shape((BLOCK, GROUP * HD), bf16),
            (info, q_rows, acc, stat, *group23),
            scratch=(pltpu.VMEM((8, BLOCK, 2 * HD), bf16),),
            flops=2 * 2048 * 1024 * 512,
            touched=4 << 20,
            exps=2 * 2048 * 1024,
            specs={
                2: pl.BlockSpec((1, GROUP, BLOCK, HD), lambda i: (side, 0, 0, 0)),
                3: pl.BlockSpec((1, BLOCK, HD), lambda i: (side, 0, 0)),
            },
        )

    out_partner = finish(q_partner, 1)
    returned = z_swap(out_partner, 1)
    out_own = finish(q_keep, 0)
    merged = call(
        merge_kernel,
        shape((rows, HD), bf16),
        (info, local_out, local_level, back0, back1),
        flops=rows * HD * 8,
        touched=1 << 20,
        exps=rows * HD * 2,
    )
    decode_out = merged.reshape(samples, steps, GROUP * HD)
    segment_out = jnp.where(
        even, jnp.stack([out_own, returned]), jnp.stack([returned, out_own])
    )
    return (segment_out[None], decode_out[None, None])


def solution(mesh):
    placed = (
        P("pd", None, "ctx", "tp"),
        P("pd", None, "ctx", "tp"),
        P("pd", "ctx", None, None, "tp"),
        P("pd", "ctx", None, None, "tp"),
        P("pd", "ctx", None, None, "tp"),
        P(),
        P(None, "tp"),
        P(),
        P("pd", "ctx", None),
    )
    return jax.shard_map(
        on_device,
        mesh=mesh,
        in_specs=placed,
        out_specs=(P("pd", None, "ctx", "tp"), P("pd", "ctx", None, None, "tp")),
        check_vma=False,
    )
```

```python
import functools

import jax
import jax.numpy as jnp
from jax import lax
from jax.experimental import pallas as pl
from jax.experimental.pallas import tpu as pltpu
from jax.sharding import PartitionSpec as P

D = 8192
HD = 128
GROUP = 8
BLOCK = 256
DECODE_ROWS = 64
MASKED = -1e30
LOG2E = 1.4426950408889634
SCALE2 = HD ** (-0.5) * LOG2E
MIB = 1024 * 1024

bf16 = jnp.bfloat16
f32 = jnp.float32


def scores_of(rows, keys):
    return lax.dot_general(rows, keys, (((1,), (1,)), ((), ())), preferred_element_type=f32)


def fill_values(aug_ref, index, block):
    aug_ref[index, :, :HD] = block[:, HD:]
    aug_ref[index, :, HD:] = jnp.ones((BLOCK, HD), bf16)


def weigh(parts, highest, aug_blocks):
    out = None
    for part, aug in zip(parts, aug_blocks):
        weights = jnp.exp2((part - highest) * SCALE2).astype(bf16)
        term = jnp.dot(weights, aug, preferred_element_type=f32)
        out = term if out is None else out + term
    return out


def max_of(parts):
    top = parts[0]
    for part in parts[1:]:
        top = jnp.maximum(top, part)
    return jnp.max(top, axis=-1, keepdims=True)


def first_kernel(info, own_q, partner_q, *refs):
    blocks = refs[:8]
    acc_ref, stat_ref, q_scr, key_scr, aug_scr = refs[8:]
    parity, row_y = info[0], info[1]
    q_scr[0] = own_q[...]
    q_scr[1] = partner_q[...]
    for group in range(2):
        for b in range(4):
            block = blocks[group * 4 + b][...]
            key_scr[group * 4 + b] = block[:, :HD]
            fill_values(aug_scr, group * 4 + b, block)
    lane = lax.broadcasted_iota(jnp.int32, (BLOCK, HD), 1)
    upper = lax.broadcasted_iota(jnp.int32, (BLOCK, BLOCK), 1) > lax.broadcasted_iota(
        jnp.int32, (BLOCK, BLOCK), 0
    )

    def shift_of(b):
        block_y = (row_y + (0, 3, 1, 2)[b]) % 4
        return jnp.where(block_y < row_y, 0.0, MASKED).astype(f32)

    for odd in (True, False):
        side = 1 - parity if odd else parity
        same = side * 4
        other = (1 - side) * 4

        def head(h, carry):
            rows = q_scr[side, :, pl.ds(pl.multiple_of(h * HD, HD), HD)]
            parts = []
            augs = []
            for b in range(4):
                part = scores_of(rows, key_scr[same + b])
                if b == 0:
                    part = jnp.where(upper, MASKED, part)
                else:
                    part = part + shift_of(b)
                parts.append(part)
                augs.append(aug_scr[same + b])
            if odd:
                for b in range(4):
                    parts.append(scores_of(rows, key_scr[other + b]))
                    augs.append(aug_scr[other + b])
            highest = max_of(parts)
            mixed = weigh(parts, highest, augs)
            acc_ref[side, h] = mixed[:, :HD]
            old = jnp.where(lane == h, highest, stat_ref[side])
            stat_ref[side] = jnp.where(lane == h + 8, mixed[:, HD:], old)
            return carry

        lax.fori_loop(0, GROUP, head, 0, unroll=4)


def last_kernel(info, q_ref, acc_ref, stat_ref, *refs):
    kv_refs = refs[:4]
    out_ref, aug_scr = refs[4:]
    lane = lax.broadcasted_iota(jnp.int32, (BLOCK, HD), 1)

    def column(h):
        return jnp.sum(jnp.where(lane == h, stat_ref[0], 0.0), axis=-1, keepdims=True)

    @pl.when(info[2] >= 2)
    def _():
        for b in range(8):
            fill_values(aug_scr, b, kv_refs[b // 2][b % 2])

        def head(h, carry):
            at = pl.ds(pl.multiple_of(h * HD, HD), HD)
            rows = q_ref[:, at]
            parts = [scores_of(rows, kv_refs[b // 2][b % 2, :, :HD]) for b in range(8)]
            before = column(h)
            highest = jnp.maximum(before, max_of(parts))
            mixed = weigh(parts, highest, [aug_scr[b] for b in range(8)])
            fade = jnp.exp2((before - highest) * SCALE2)
            total = column(h + 8) * fade + mixed[:, HD:]
            out_ref[:, at] = ((acc_ref[0, h] * fade + mixed[:, :HD]) / total).astype(bf16)
            return carry

        lax.fori_loop(0, GROUP, head, 0, unroll=4)

    @pl.when(info[2] < 2)
    def _():
        def head(h, carry):
            at = pl.ds(pl.multiple_of(h * HD, HD), HD)
            out_ref[:, at] = (acc_ref[0, h] / column(h + 8)).astype(bf16)
            return carry

        lax.fori_loop(0, GROUP, head, 0)


def segment_kernel(info, rows_ref, *refs):
    near = refs[:8]
    far = refs[8:12]
    out_ref, aug_scr = refs[12:]

    def block_of(b, at):
        if b < 8:
            return near[b][:, at]
        return far[(b - 8) // 2][(b - 8) % 2, :, at]

    for b in range(16):
        aug_scr[b, :, :HD] = block_of(b, slice(HD, 2 * HD))
        aug_scr[b, :, HD:] = jnp.ones((BLOCK, HD), bf16)
    lane = lax.broadcasted_iota(jnp.int32, (DECODE_ROWS, HD), 1)

    for which in range(2):

        @pl.when(info[3 + which] == 1)
        def _():
            stat = jnp.zeros((DECODE_ROWS, HD), f32)
            for tile in range(2):
                heads = range(tile * 4, tile * 4 + 4)
                rows = jnp.concatenate(
                    [rows_ref[which, :, h * HD : (h + 1) * HD] for h in heads], axis=0
                )
                highest = None
                for chunk in range(4):
                    blocks = range(chunk * 4, chunk * 4 + 4)
                    parts = [scores_of(rows, block_of(b, slice(0, HD))) for b in blocks]
                    top = max_of(parts)
                    if highest is None:
                        mixed = weigh(parts, top, [aug_scr[b] for b in blocks])
                    else:
                        top = jnp.maximum(top, highest)
                        mixed = mixed * jnp.exp2((highest - top) * SCALE2) + weigh(
                            parts, top, [aug_scr[b] for b in blocks]
                        )
                    highest = top
                total = mixed[:, HD:]
                share = (mixed[:, :HD] / total).astype(bf16)
                level = highest * SCALE2 + jnp.log2(total)
                for i, h in enumerate(heads):
                    at = slice(i * DECODE_ROWS, (i + 1) * DECODE_ROWS)
                    out_ref[which, :, h * HD : (h + 1) * HD] = share[at]
                    stat = jnp.where(lane == h, level[at], stat)
            high = stat.astype(bf16).astype(f32)
            middle = (stat - high).astype(bf16).astype(f32)
            low = stat - high - middle
            pieces = high + pltpu.roll(middle, 8, 1) + pltpu.roll(low, 16, 1)
            out_ref[which, :, GROUP * HD :] = pieces.astype(bf16)

        @pl.when(info[3 + which] != 1)
        def _():
            out_ref[which] = jnp.zeros((DECODE_ROWS, (GROUP + 1) * HD), bf16)


def local_kernel(
    info, len_ref, cos_ref, sin_ref, gain_ref, q_ref, near_ref, far_ref, weight_ref, cache_ref,
    out_ref, level_ref,
):
    width = near_ref.shape[2]
    core, x = info[6], info[7]
    squares = jnp.zeros((DECODE_ROWS, 1), f32)
    projected = jnp.zeros((DECODE_ROWS, 2 * HD), f32)
    for side, part_ref in enumerate((near_ref, far_ref)):
        for i, step in enumerate((0, 3, 1, 2)):
            owner = ((x + step) % 4) * 2 + (core if side == 0 else 1 - core)
            wide = part_ref[i].astype(f32)
            squares = squares + jnp.sum(wide * wide, axis=-1, keepdims=True)
            scaled = (wide * gain_ref[pl.ds(owner, 1)]).astype(bf16)
            projected = projected + jnp.dot(
                scaled,
                weight_ref[pl.ds(pl.multiple_of(owner * width, width), width)],
                preferred_element_type=f32,
            )
    normed = projected * lax.rsqrt(squares / D + 1e-6)
    key_rows = normed[:, :HD]
    turned = pltpu.roll(key_rows, HD // 2, 1)
    fresh_k = (key_rows * cos_ref[...] + turned * sin_ref[...]).astype(bf16)
    fresh_v = normed[:, HD:].astype(bf16)
    fresh_aug = jnp.concatenate([fresh_v, jnp.ones((DECODE_ROWS, HD), bf16)], axis=1)
    ones = jnp.ones((BLOCK, HD), bf16)
    row = lax.broadcasted_iota(jnp.int32, (128, BLOCK), 0)
    slot = lax.broadcasted_iota(jnp.int32, (128, BLOCK), 1)
    fresh_row = lax.broadcasted_iota(jnp.int32, (128, DECODE_ROWS), 0) % 16
    fresh_slot = lax.broadcasted_iota(jnp.int32, (128, DECODE_ROWS), 1)

    for g in range(4):
        at = slice(g * 16, (g + 1) * 16)
        rows = jnp.concatenate([q_ref[at, h * HD : (h + 1) * HD] for h in range(GROUP)], axis=0)
        parts = []
        augs = []
        for j in range(4):
            s = g * 4 + j
            allowed = (row % 16 // 4 == j) & (slot < len_ref[s])
            parts.append(jnp.where(allowed, scores_of(rows, cache_ref[s, :, :HD]), MASKED))
            augs.append(jnp.concatenate([cache_ref[s, :, HD:], ones], axis=1))
        behind = fresh_row + g * 16 - fresh_slot
        allowed = (behind >= 0) & (behind <= fresh_row % 4)
        fresh_part = jnp.where(allowed, scores_of(rows, fresh_k), MASKED)
        highest = jnp.maximum(max_of(parts), jnp.max(fresh_part, axis=-1, keepdims=True))
        mixed = weigh(parts + [fresh_part], highest, augs + [fresh_aug])
        total = mixed[:, HD:]
        share = mixed[:, :HD] / total
        level = highest * SCALE2 + jnp.log2(total)
        for h in range(GROUP):
            out_ref[at, h * HD : (h + 1) * HD] = share[h * 16 : (h + 1) * 16]
            level_ref[at, h * HD : (h + 1) * HD] = level[h * 16 : (h + 1) * 16]


def merge_kernel(info, local_ref, level_ref, same_ref, other_ref, out_ref):
    lane = lax.broadcasted_iota(jnp.int32, (DECODE_ROWS, HD), 1)

    def merge(part_ref):
        pieces = part_ref[:, GROUP * HD :].astype(f32)
        for h in range(GROUP):
            at = slice(h * HD, (h + 1) * HD)
            mine = (lane == h) | (lane == h + 8) | (lane == h + 16)
            far = jnp.sum(jnp.where(mine, pieces, 0.0), axis=-1, keepdims=True)
            near = level_ref[:, at]
            top = jnp.maximum(far, near)
            far_share = jnp.exp2(far - top)
            near_share = jnp.exp2(near - top)
            mixed = part_ref[:, at].astype(f32) * far_share + local_ref[:, at] * near_share
            out_ref[:, at] = (mixed / (far_share + near_share)).astype(bf16)

    @pl.when(info[5] == 1)
    def _():
        merge(same_ref)

    @pl.when(info[5] != 1)
    def _():
        merge(other_ref)


SMEM = pl.BlockSpec(memory_space=pltpu.SMEM)
VMEM = pl.BlockSpec(memory_space=pltpu.VMEM)


def call(kernel, out_shape, args, scalars=1, scratch=(), flops=0, touched=0, exps=0, specs=None, vmem=24):
    in_specs = [SMEM] * scalars + [VMEM] * (len(args) - scalars)
    for place, spec in (specs or {}).items():
        in_specs[place] = spec
    return pl.pallas_call(
        kernel,
        grid=(1,) if specs else (),
        out_shape=out_shape,
        in_specs=in_specs,
        out_specs=jax.tree.map(lambda _: VMEM, out_shape),
        scratch_shapes=list(scratch),
        compiler_params=pltpu.CompilerParams(vmem_limit_bytes=vmem * MIB),
        cost_estimate=pl.CostEstimate(flops=flops, bytes_accessed=touched, transcendentals=exps),
    )(*args)


def y_turn(block, distance):
    route = [(i, i // 4 * 4 + (i % 4 + distance) % 4) for i in range(16)]
    return lax.ppermute(block, "ctx", route)


def z_swap(block, bits):
    return lax.ppermute(block, "ctx", [(i, i ^ (4 * bits)) for i in range(16)])


def y_all(block):
    return [block, y_turn(block, 1), y_turn(block, -1), y_turn(block, 2)]


def tp_turn(block, distance):
    return lax.ppermute(block, "tp", [(i, (i + distance) % 8) for i in range(8)])


def pool_swap(block, z_bits):
    route = [(i, (i ^ 1) ^ (8 * z_bits)) for i in range(32)]
    return lax.ppermute(block, ("ctx", "pd"), route)


def on_device(
    prefill_query,
    prefill_kv,
    decode_query,
    gen_cache,
    new_hidden,
    norm_gain,
    kv_weight,
    prompt_of,
    cached_len,
):
    queries = prefill_query[0]
    keyvals = prefill_kv[0]
    place = lax.axis_index("ctx")
    pool = lax.axis_index("pd")
    z, y = place // 4, place % 4
    parity = z % 2
    here = lax.dynamic_index_in_dim(prompt_of, pool, 0, keepdims=False)
    there = lax.dynamic_index_in_dim(prompt_of, 1 - pool, 0, keepdims=False)
    info = jnp.stack(
        [
            parity,
            y,
            z,
            (here[place] == parity).astype(jnp.int32),
            (here[place ^ 4] == parity).astype(jnp.int32),
            (there[place] == parity).astype(jnp.int32),
            lax.axis_index("tp") % 2,
            lax.axis_index("tp") // 2,
        ]
    ).astype(jnp.int32)

    even = parity == 0
    kv_keep = jnp.where(even, keyvals[0], keyvals[1])
    kv_give = jnp.where(even, keyvals[1], keyvals[0])
    from_z1 = z_swap(kv_give, 1)
    from_z2 = z_swap(kv_keep, 2)
    from_z3 = z_swap(kv_give, 3)
    group0 = y_all(kv_keep)
    q_keep = jnp.where(even, queries[0], queries[1])
    q_give = jnp.where(even, queries[1], queries[0])
    q_partner = z_swap(q_give, 1)
    group1 = y_all(from_z1)
    group23 = y_all(jnp.stack([from_z2, from_z3]))

    hidden = new_hidden[0, 0]
    samples, steps, width = hidden.shape
    decode_rows = samples * steps
    hidden = hidden.reshape(decode_rows, width)
    near = jnp.stack([hidden, tp_turn(hidden, 2), tp_turn(hidden, -2), tp_turn(hidden, 4)])
    far = lax.ppermute(near, "tp", [(i, i ^ 1) for i in range(8)])
    step_rows = decode_query[0, 0].reshape(decode_rows, width)
    rows_pair = pool_swap(jnp.stack([step_rows, z_swap(step_rows, 1)]), 0)

    lengths = cached_len[0, 0]
    half = HD // 2
    frequency = 1000000.0 ** (-jnp.arange(half, dtype=f32) * 2.0 / HD)
    positions = (4096 + lengths[:, None] + jnp.arange(steps, dtype=jnp.int32)[None, :]).astype(f32)
    angles = positions.reshape(-1)[:, None] * frequency
    cosine, sine = jnp.cos(angles), jnp.sin(angles)
    cos_all = jnp.concatenate([cosine, cosine], axis=-1)
    sin_all = jnp.concatenate([-sine, sine], axis=-1)

    shape = jax.ShapeDtypeStruct
    local_out, local_level = call(
        local_kernel,
        (shape((decode_rows, width), f32), shape((decode_rows, width), f32)),
        (
            info,
            lengths,
            cos_all,
            sin_all,
            norm_gain.reshape(D // width, width),
            step_rows,
            near,
            far,
            kv_weight,
            gen_cache[0, 0],
        ),
        scalars=2,
        flops=2 * 64 * D * 256,
        touched=8 << 20,
        exps=512 * 320,
    )

    acc, stat = call(
        first_kernel,
        (shape((2, GROUP, BLOCK, HD), f32), shape((2, BLOCK, HD), f32)),
        (info, q_keep, q_partner, *group0, *group1),
        scratch=(
            pltpu.VMEM((2, BLOCK, GROUP * HD), bf16),
            pltpu.VMEM((8, BLOCK, HD), bf16),
            pltpu.VMEM((8, BLOCK, 2 * HD), bf16),
        ),
        flops=3 * 2048 * 1024 * 512,
        touched=4 << 20,
        exps=3 * 2048 * 1024,
    )
    segment_pair = call(
        segment_kernel,
        shape((2, decode_rows, width + HD), bf16),
        (info, rows_pair, *group0, *group1, *group23),
        scratch=(pltpu.VMEM((16, BLOCK, 2 * HD), bf16),),
        flops=1024 * 4096 * 512,
        touched=3 << 20,
        exps=1024 * 4096,
    )
    back0 = pool_swap(segment_pair[0], 0)
    back1 = pool_swap(segment_pair[1], 1)

    def finish(q_rows, side):
        return call(
            last_kernel,
            shape((BLOCK, GROUP * HD), bf16),
            (info, q_rows, acc, stat, *group23),
            scratch=(pltpu.VMEM((8, BLOCK, 2 * HD), bf16),),
            flops=2 * 2048 * 1024 * 512,
            touched=4 << 20,
            exps=2 * 2048 * 1024,
            specs={
                2: pl.BlockSpec((1, GROUP, BLOCK, HD), lambda i: (side, 0, 0, 0)),
                3: pl.BlockSpec((1, BLOCK, HD), lambda i: (side, 0, 0)),
            },
        )

    out_partner = finish(q_partner, 1)
    returned = z_swap(out_partner, 1)
    out_own = finish(q_keep, 0)
    merged = call(
        merge_kernel,
        shape((decode_rows, width), bf16),
        (info, local_out, local_level, back0, back1),
        flops=512 * HD * 8,
        touched=1 << 20,
        exps=512 * HD * 2,
    )
    decode_out = merged.reshape(samples, steps, width)
    segment_out = jnp.where(
        even, jnp.stack([out_own, returned]), jnp.stack([returned, out_own])
    )
    return (segment_out[None], decode_out[None, None])


def solution(mesh):
    placed = (
        P("pd", None, "ctx", "tp"),
        P("pd", None, "ctx", "tp"),
        P("pd", "ctx", None, None, "tp"),
        P("pd", "ctx", None, None, "tp"),
        P("pd", "ctx", None, None, "tp"),
        P(),
        P(None, "tp"),
        P(),
        P("pd", "ctx", None),
    )
    return jax.shard_map(
        on_device,
        mesh=mesh,
        in_specs=placed,
        out_specs=(P("pd", None, "ctx", "tp"), P("pd", "ctx", None, None, "tp")),
        check_vma=False,
    )
```

```python
import functools

import jax
import jax.numpy as jnp
from jax import lax
from jax.experimental import pallas as pl
from jax.experimental.pallas import tpu as pltpu
from jax.sharding import PartitionSpec as P

D = 8192
HD = 128
GROUP = 8
BLOCK = 256
DECODE_ROWS = 64
MASKED = -1e30
LOG2E = 1.4426950408889634
SCALE2 = HD ** (-0.5) * LOG2E
MIB = 1024 * 1024

bf16 = jnp.bfloat16
f32 = jnp.float32


def scores_of(rows, keys):
    return lax.dot_general(rows, keys, (((1,), (1,)), ((), ())), preferred_element_type=f32)


def place():
    index = lax.axis_index("ctx")
    return index // 4, index % 4, index // 4 % 2


def fill_values(aug_ref, index, block):
    aug_ref[index, :, :HD] = block[:, HD:]
    aug_ref[index, :, HD:] = jnp.ones((BLOCK, HD), bf16)


def weigh(parts, highest, aug_blocks):
    out = None
    for part, aug in zip(parts, aug_blocks):
        weights = jnp.exp2((part - highest) * SCALE2).astype(bf16)
        term = jnp.dot(weights, aug, preferred_element_type=f32)
        out = term if out is None else out + term
    return out


def max_of(parts):
    top = parts[0]
    for part in parts[1:]:
        top = jnp.maximum(top, part)
    return jnp.max(top, axis=-1, keepdims=True)


def flatten(target_ref, source_ref):
    for s in range(16):
        target_ref[s * 4 : s * 4 + 4] = source_ref[s]


def first_kernel(own_q, partner_q, hidden_in, rows_in, *refs):
    blocks = refs[:4]
    acc_ref, stat_ref, hidden_ref, rows_ref, aug_scr = refs[4:]
    flatten(hidden_ref, hidden_in)
    flatten(rows_ref, rows_in)
    _, row_y, parity = place()
    for group in range(2):
        for b in range(4):
            fill_values(aug_scr, group * 4 + b, blocks[b][group])
    lane = lax.broadcasted_iota(jnp.int32, (BLOCK, HD), 1)
    upper = lax.broadcasted_iota(jnp.int32, (BLOCK, BLOCK), 1) > lax.broadcasted_iota(
        jnp.int32, (BLOCK, BLOCK), 0
    )

    def shift_of(b):
        block_y = (row_y + (0, 3, 1, 2)[b]) % 4
        return jnp.where(block_y < row_y, 0.0, MASKED).astype(f32)

    for odd in (True, False):
        side = 1 - parity if odd else parity
        same = side * 4
        other = (1 - side) * 4

        def head(h, carry):
            at = pl.ds(pl.multiple_of(h * HD, HD), HD)
            rows = jnp.where(side == 0, own_q[parity, :, at], partner_q[:, at])
            parts = []
            augs = []
            for b in range(4):
                part = scores_of(rows, blocks[b][side, :, :HD])
                if b == 0:
                    part = jnp.where(upper, MASKED, part)
                else:
                    part = part + shift_of(b)
                parts.append(part)
                augs.append(aug_scr[same + b])
            if odd:
                for b in range(4):
                    parts.append(scores_of(rows, blocks[b][1 - side, :, :HD]))
                    augs.append(aug_scr[other + b])
            highest = max_of(parts)
            mixed = weigh(parts, highest, augs)
            acc_ref[side, h] = mixed[:, :HD]
            old = jnp.where(lane == h, highest, stat_ref[side])
            stat_ref[side] = jnp.where(lane == h + 8, mixed[:, HD:], old)
            return carry

        lax.fori_loop(0, GROUP, head, 0, unroll=4)


def last_kernel(own, q_ref, acc_ref, stat_ref, *refs):
    kv_refs = refs[:4]
    out_ref, extra_ref, aug_scr, out_scr, sems = refs[-5:]
    if own:
        extra_ref[...] = jnp.zeros_like(extra_ref)
    else:
        extra_ref[0] = refs[4][...]
        extra_ref[1] = refs[5][...]
    z, _, parity = place()
    side = 0 if own else 1
    if own:
        q_ref = q_ref.at[parity]
        out_ref = out_ref.at[parity]
    lane = lax.broadcasted_iota(jnp.int32, (BLOCK, HD), 1)

    def column(h):
        return jnp.sum(jnp.where(lane == h, stat_ref[side], 0.0), axis=-1, keepdims=True)

    def copy_of(half):
        at = pl.ds(pl.multiple_of(half * 4 * HD, 4 * HD), 4 * HD)
        return pltpu.make_async_copy(out_scr.at[:, at], out_ref.at[:, at], sems.at[half])

    def halves(head):
        def step(half, carry):
            for i in range(4):
                head(half * 4 + i)
            copy_of(half).start()
            return carry

        lax.fori_loop(0, 2, step, 0)

    @pl.when(z >= 2)
    def _():
        for b in range(8):
            fill_values(aug_scr, b, kv_refs[b // 2][b % 2])

        def head(h):
            at = pl.ds(pl.multiple_of(h * HD, HD), HD)
            rows = q_ref[:, at]
            parts = [scores_of(rows, kv_refs[b // 2][b % 2, :, :HD]) for b in range(8)]
            before = column(h)
            highest = jnp.maximum(before, max_of(parts))
            mixed = weigh(parts, highest, [aug_scr[b] for b in range(8)])
            fade = jnp.exp2((before - highest) * SCALE2)
            total = column(h + 8) * fade + mixed[:, HD:]
            out_scr[:, at] = ((acc_ref[side, h] * fade + mixed[:, :HD]) / total).astype(bf16)

        halves(head)

    @pl.when(z < 2)
    def _():
        def head(h):
            at = pl.ds(pl.multiple_of(h * HD, HD), HD)
            out_scr[:, at] = (acc_ref[side, h] / column(h + 8)).astype(bf16)

        halves(head)

    for half in range(2):
        copy_of(half).wait()


def segment_kernel(prompt_ref, _, rows0_ref, rows1_ref, *refs):
    kv_refs = refs[:8]
    out0_ref, out1_ref, done_ref, aug_scr = refs[-4:]
    done_ref[...] = jnp.zeros_like(done_ref)
    index, pool = lax.axis_index("ctx"), lax.axis_index("pd")
    parity = place()[2]

    def block_of(b, at):
        return kv_refs[b // 2][b % 2, :, at]

    for b in range(16):
        aug_scr[b, :, :HD] = block_of(b, slice(HD, 2 * HD))
        aug_scr[b, :, HD:] = jnp.ones((BLOCK, HD), bf16)
    lane = lax.broadcasted_iota(jnp.int32, (DECODE_ROWS, HD), 1)

    for which, rows_ref, out_ref in ((0, rows0_ref, out0_ref), (1, rows1_ref, out1_ref)):
        needed = prompt_ref[pool, index ^ (4 * which)] == parity

        @pl.when(needed)
        def _():
            stat = jnp.zeros((DECODE_ROWS, HD), f32)
            for tile in range(2):
                heads = range(tile * 4, tile * 4 + 4)
                rows = jnp.concatenate(
                    [rows_ref[:, h * HD : (h + 1) * HD] for h in heads], axis=0
                )
                highest = None
                for chunk in range(4):
                    blocks = range(chunk * 4, chunk * 4 + 4)
                    parts = [scores_of(rows, block_of(b, slice(0, HD))) for b in blocks]
                    top = max_of(parts)
                    if highest is None:
                        mixed = weigh(parts, top, [aug_scr[b] for b in blocks])
                    else:
                        top = jnp.maximum(top, highest)
                        mixed = mixed * jnp.exp2((highest - top) * SCALE2) + weigh(
                            parts, top, [aug_scr[b] for b in blocks]
                        )
                    highest = top
                total = mixed[:, HD:]
                share = (mixed[:, :HD] / total).astype(bf16)
                level = highest * SCALE2 + jnp.log2(total)
                for i, h in enumerate(heads):
                    at = slice(i * DECODE_ROWS, (i + 1) * DECODE_ROWS)
                    out_ref[:, h * HD : (h + 1) * HD] = share[at]
                    stat = jnp.where(lane == h, level[at], stat)
            high = stat.astype(bf16).astype(f32)
            middle = (stat - high).astype(bf16).astype(f32)
            low = stat - high - middle
            pieces = high + pltpu.roll(middle, 8, 1) + pltpu.roll(low, 16, 1)
            out_ref[:, GROUP * HD :] = pieces.astype(bf16)

        @pl.when(jnp.logical_not(needed))
        def _():
            out_ref[...] = jnp.zeros_like(out_ref)


def local_kernel(
    len_ref, _, cos_ref, sin_ref, gain_ref, q_ref, own_ref, twin_ref, *refs
):
    pairs = refs[:3]
    weight_ref, cache_ref = refs[3:5]
    out_ref, level_ref = refs[-2:]
    width = own_ref.shape[1]
    core, x = lax.axis_index("tp") % 2, lax.axis_index("tp") // 2
    squares = jnp.zeros((DECODE_ROWS, 1), f32)
    projected = jnp.zeros((DECODE_ROWS, 2 * HD), f32)
    for i, step in enumerate((0, 3, 1, 2)):
        for side in range(2):
            owner = ((x + step) % 4) * 2 + (core if side == 0 else 1 - core)
            if i == 0:
                wide = (own_ref, twin_ref)[side][...].astype(f32)
            else:
                wide = pairs[i - 1][side].astype(f32)
            at = pl.ds(pl.multiple_of(owner * width, width), width)
            squares = squares + jnp.sum(wide * wide, axis=-1, keepdims=True)
            scaled = (wide * gain_ref[:, at]).astype(bf16)
            projected = projected + jnp.dot(
                scaled, weight_ref[at], preferred_element_type=f32
            )
    normed = projected * lax.rsqrt(squares / D + 1e-6)
    key_rows = normed[:, :HD]
    turned = pltpu.roll(key_rows, HD // 2, 1)
    fresh_k = (key_rows * cos_ref[...] + turned * sin_ref[...]).astype(bf16)
    fresh_v = normed[:, HD:].astype(bf16)
    fresh_aug = jnp.concatenate([fresh_v, jnp.ones((DECODE_ROWS, HD), bf16)], axis=1)
    ones = jnp.ones((BLOCK, HD), bf16)
    row = lax.broadcasted_iota(jnp.int32, (128, BLOCK), 0)
    slot = lax.broadcasted_iota(jnp.int32, (128, BLOCK), 1)
    fresh_row = lax.broadcasted_iota(jnp.int32, (128, DECODE_ROWS), 0) % 16
    fresh_slot = lax.broadcasted_iota(jnp.int32, (128, DECODE_ROWS), 1)

    for g in range(4):
        at = slice(g * 16, (g + 1) * 16)
        rows = jnp.concatenate([q_ref[at, h * HD : (h + 1) * HD] for h in range(GROUP)], axis=0)
        parts = []
        augs = []
        for j in range(4):
            s = g * 4 + j
            allowed = (row % 16 // 4 == j) & (slot < len_ref[s])
            parts.append(jnp.where(allowed, scores_of(rows, cache_ref[s, :, :HD]), MASKED))
            augs.append(jnp.concatenate([cache_ref[s, :, HD:], ones], axis=1))
        behind = fresh_row + g * 16 - fresh_slot
        allowed = (behind >= 0) & (behind <= fresh_row % 4)
        fresh_part = jnp.where(allowed, scores_of(rows, fresh_k), MASKED)
        highest = jnp.maximum(max_of(parts), jnp.max(fresh_part, axis=-1, keepdims=True))
        mixed = weigh(parts + [fresh_part], highest, augs + [fresh_aug])
        total = mixed[:, HD:]
        share = mixed[:, :HD] / total
        level = highest * SCALE2 + jnp.log2(total)
        for h in range(GROUP):
            out_ref[at, h * HD : (h + 1) * HD] = share[h * 16 : (h + 1) * 16]
            level_ref[at, h * HD : (h + 1) * HD] = level[h * 16 : (h + 1) * 16]


def merge_kernel(
    prompt_ref, local_ref, level_ref, same_ref, other_ref, returned_ref, own_out, out_ref, full_ref,
    sem,
):
    del own_out
    parity = place()[2]
    copy = pltpu.make_async_copy(returned_ref, full_ref.at[1 - parity], sem)
    copy.start()
    lane = lax.broadcasted_iota(jnp.int32, (DECODE_ROWS, HD), 1)
    held_here = prompt_ref[1 - lax.axis_index("pd"), lax.axis_index("ctx")] == parity

    def merge(part_ref):
        pieces = part_ref[:, GROUP * HD :].astype(f32)
        for h in range(GROUP):
            at = slice(h * HD, (h + 1) * HD)
            mine = (lane == h) | (lane == h + 8) | (lane == h + 16)
            far = jnp.sum(jnp.where(mine, pieces, 0.0), axis=-1, keepdims=True)
            near = level_ref[:, at]
            top = jnp.maximum(far, near)
            far_share = jnp.exp2(far - top)
            near_share = jnp.exp2(near - top)
            mixed = part_ref[:, at].astype(f32) * far_share + local_ref[:, at] * near_share
            merged = mixed / (far_share + near_share)
            for s in range(16):
                out_ref[s, :, at] = merged[s * 4 : s * 4 + 4].astype(bf16)

    @pl.when(held_here)
    def _():
        merge(same_ref)

    @pl.when(jnp.logical_not(held_here))
    def _():
        merge(other_ref)

    copy.wait()


SMEM = pl.BlockSpec(memory_space=pltpu.SMEM)
VMEM = pl.BlockSpec(memory_space=pltpu.VMEM)
ANY = pl.BlockSpec(memory_space=pl.ANY)


def call(
    kernel, out_shape, args, scalars=0, scratch=(), flops=0, touched=0, exps=0, specs=None,
    out_specs=None, aliases=None, vmem=14,
):
    in_specs = [SMEM] * scalars + [VMEM] * (len(args) - scalars)
    for at, spec in (specs or {}).items():
        in_specs[at] = spec
    return pl.pallas_call(
        kernel,
        out_shape=out_shape,
        in_specs=in_specs,
        out_specs=out_specs or jax.tree.map(lambda _: VMEM, out_shape),
        scratch_shapes=list(scratch),
        input_output_aliases=aliases or {},
        compiler_params=pltpu.CompilerParams(vmem_limit_bytes=vmem * MIB),
        cost_estimate=pl.CostEstimate(flops=flops, bytes_accessed=touched, transcendentals=exps),
    )(*args)


def after(value, *others):
    return lax.optimization_barrier((value, *others))[0]


def y_turn(block, distance):
    route = [(i, i // 4 * 4 + (i % 4 + distance) % 4) for i in range(16)]
    return lax.ppermute(block, "ctx", route)


def z_swap(block, bits):
    return lax.ppermute(block, "ctx", [(i, i ^ (4 * bits)) for i in range(16)])


def y_all(block):
    return [block, y_turn(block, 1), y_turn(block, -1), y_turn(block, 2)]


def tp_turn(block, distance):
    return lax.ppermute(block, "tp", [(i, (i + distance) % 8) for i in range(8)])


def pool_swap(block, z_bits):
    route = [(i, (i ^ 1) ^ (8 * z_bits)) for i in range(32)]
    return lax.ppermute(block, ("ctx", "pd"), route)


def on_device(
    prefill_query,
    prefill_kv,
    decode_query,
    gen_cache,
    new_hidden,
    norm_gain,
    kv_weight,
    prompt_of,
    cached_len,
):
    queries = prefill_query[0]
    keyvals = prefill_kv[0]
    even = lax.axis_index("ctx") // 4 % 2 == 0
    shape = jax.ShapeDtypeStruct

    kv_keep = jnp.where(even, keyvals[0], keyvals[1])
    kv_give = jnp.where(even, keyvals[1], keyvals[0])
    from_z1 = z_swap(kv_give, 1)
    from_z2 = z_swap(kv_keep, 2)
    from_z3 = z_swap(kv_give, 3)
    q_give = lax.dynamic_index_in_dim(queries, even.astype(jnp.int32), 0, keepdims=False)
    samples, steps, width = new_hidden.shape[2:]
    decode_rows = samples * steps
    from_z1, q_give = lax.optimization_barrier((from_z1, q_give))
    first_pair, q_give = lax.optimization_barrier((jnp.stack([kv_keep, from_z1]), q_give))
    group01 = y_all(first_pair)
    q_partner = z_swap(q_give, 1)
    group23 = y_all(jnp.stack([from_z2, from_z3]))

    lengths = cached_len[0, 0]
    half = HD // 2
    frequency = 1000000.0 ** (-jnp.arange(half, dtype=f32) * 2.0 / HD)
    positions = (4096 + lengths[:, None] + jnp.arange(steps, dtype=jnp.int32)[None, :]).astype(f32)
    angles = positions.reshape(-1)[:, None] * frequency
    cosine, sine = jnp.cos(angles), jnp.sin(angles)
    cos_all = jnp.concatenate([cosine, cosine], axis=-1)
    sin_all = jnp.concatenate([-sine, sine], axis=-1)

    token = shape((8, HD), f32)
    flat = shape((decode_rows, width), bf16)
    acc, stat, hidden, step_rows = call(
        first_kernel,
        (shape((2, GROUP, BLOCK, HD), f32), shape((2, BLOCK, HD), f32), flat, flat),
        (queries, q_partner, new_hidden[0, 0], decode_query[0, 0], *group01),
        scratch=(
            pltpu.VMEM((8, BLOCK, 2 * HD), bf16),
        ),
        flops=3 * 2048 * 1024 * 512,
        touched=4 << 20,
        exps=3 * 2048 * 1024,
    )
    twin = lax.ppermute(hidden, "tp", [(i, i ^ 1) for i in range(8)])
    rows_pair = [pool_swap(step_rows, 0), pool_swap(step_rows, 1)]

    def finish(own, q_rows, extra):
        out_rows = (BLOCK, GROUP * HD)
        last = token if own else shape((2, decode_rows, width), bf16)
        return call(
            functools.partial(last_kernel, own),
            (shape((2, *out_rows) if own else out_rows, bf16), last),
            (q_rows, acc, stat, *group23, *extra),
            scratch=(
                pltpu.VMEM((8, BLOCK, 2 * HD), bf16),
                pltpu.VMEM(out_rows, bf16),
                pltpu.SemaphoreType.DMA((2,)),
            ),
            specs={7: ANY} if own else None,
            out_specs=(ANY, VMEM),
            flops=2 * 2048 * 1024 * 512,
            touched=4 << 20,
            exps=2 * 2048 * 1024,
        )

    out_partner, pair = finish(False, q_partner, (hidden, twin))
    returned = z_swap(out_partner, 1)
    pairs = [tp_turn(pair, 2), tp_turn(pair, -2), tp_turn(pair, 4)]
    part = shape((decode_rows, width + HD), bf16)
    segment0, segment1, segment_done = call(
        segment_kernel,
        (part, part, token),
        (prompt_of, pair, *rows_pair, *group01, *group23),
        specs={1: ANY},
        scalars=1,
        scratch=(pltpu.VMEM((16, BLOCK, 2 * HD), bf16),),
        flops=1024 * 4096 * 512,
        touched=3 << 20,
        exps=1024 * 4096,
    )
    back0 = pool_swap(segment0, 0)
    back1 = pool_swap(segment1, 1)
    out_own, own_done = finish(True, queries, (segment_done,))
    local_out, local_level = call(
        local_kernel,
        (shape((decode_rows, width), f32), shape((decode_rows, width), f32)),
        (
            lengths,
            own_done,
            cos_all,
            sin_all,
            norm_gain[None],
            step_rows,
            hidden,
            twin,
            *pairs,
            kv_weight,
            gen_cache[0, 0],
        ),
        scalars=1,
        specs={1: ANY},
        flops=2 * 64 * D * 256,
        touched=8 << 20,
        exps=512 * 320,
    )

    merged, segment_out = call(
        merge_kernel,
        (shape((samples, steps, width), bf16), shape(queries.shape, bf16)),
        (prompt_of, local_out, local_level, back0, back1, returned, out_own),
        scalars=1,
        scratch=(pltpu.SemaphoreType.DMA,),
        flops=512 * HD * 8,
        touched=1 << 20,
        exps=512 * HD * 2,
        specs={5: ANY, 6: ANY},
        out_specs=(VMEM, ANY),
        aliases={6: 1},
        vmem=8,
    )
    return (segment_out[None], merged[None, None])


def solution(mesh):
    placed = (
        P("pd", None, "ctx", "tp"),
        P("pd", None, "ctx", "tp"),
        P("pd", "ctx", None, None, "tp"),
        P("pd", "ctx", None, None, "tp"),
        P("pd", "ctx", None, None, "tp"),
        P(),
        P(None, "tp"),
        P(),
        P("pd", "ctx", None),
    )
    return jax.shard_map(
        on_device,
        mesh=mesh,
        in_specs=placed,
        out_specs=(P("pd", None, "ctx", "tp"), P("pd", "ctx", None, None, "tp")),
        check_vma=False,
    )
```

```python
import functools

import jax
import jax.numpy as jnp
from jax import lax
from jax.experimental import pallas as pl
from jax.experimental.pallas import tpu as pltpu
from jax.sharding import PartitionSpec as P

D = 8192
HD = 128
GROUP = 8
BLOCK = 256
DECODE_ROWS = 64
MASKED = -1e30
LOG2E = 1.4426950408889634
SCALE2 = HD ** (-0.5) * LOG2E
MIB = 1024 * 1024

bf16 = jnp.bfloat16
f32 = jnp.float32


def scores_of(rows, keys):
    return lax.dot_general(rows, keys, (((1,), (1,)), ((), ())), preferred_element_type=f32)


def place():
    index = lax.axis_index("ctx")
    return index // 4, index % 4, index // 4 % 2


def fill_values(aug_ref, index, block):
    aug_ref[index, :, :HD] = block[:, HD:]
    aug_ref[index, :, HD:] = jnp.ones((BLOCK, HD), bf16)


def weigh(parts, highest, aug_blocks):
    out = None
    for part, aug in zip(parts, aug_blocks):
        weights = jnp.exp2((part - highest) * SCALE2).astype(bf16)
        term = jnp.dot(weights, aug, preferred_element_type=f32)
        out = term if out is None else out + term
    return out


def max_of(parts):
    top = parts[0]
    for part in parts[1:]:
        top = jnp.maximum(top, part)
    return jnp.max(top, axis=-1, keepdims=True)


def in_turn(steps):
    parts = steps[0][0]()
    for i, (_, finish) in enumerate(steps):
        following = steps[i + 1][0]() if i + 1 < len(steps) else None
        finish(parts)
        parts = following


def flatten(target_ref, source_ref):
    for s in range(16):
        target_ref[s * 4 : s * 4 + 4] = source_ref[s]


def first_kernel(own_q, partner_q, hidden_in, rows_in, *refs):
    blocks = refs[:4]
    acc_ref, stat_ref, hidden_ref, rows_ref, aug_scr = refs[4:]
    flatten(hidden_ref, hidden_in)
    flatten(rows_ref, rows_in)
    _, row_y, parity = place()
    for group in range(2):
        for b in range(4):
            fill_values(aug_scr, group * 4 + b, blocks[b][group])
    lane = lax.broadcasted_iota(jnp.int32, (BLOCK, HD), 1)
    upper = lax.broadcasted_iota(jnp.int32, (BLOCK, BLOCK), 1) > lax.broadcasted_iota(
        jnp.int32, (BLOCK, BLOCK), 0
    )

    def shift_of(b):
        block_y = (row_y + (0, 3, 1, 2)[b]) % 4
        return jnp.where(block_y < row_y, 0.0, MASKED).astype(f32)

    def step(odd, h):
        side = 1 - parity if odd else parity
        at = slice(h * HD, (h + 1) * HD)

        def score():
            rows = jnp.where(side == 0, own_q[parity, :, at], partner_q[:, at])
            parts = []
            for b in range(4):
                part = scores_of(rows, blocks[b][side, :, :HD])
                if b == 0:
                    parts.append(jnp.where(upper, MASKED, part))
                else:
                    parts.append(part + shift_of(b))
            if odd:
                parts += [scores_of(rows, blocks[b][1 - side, :, :HD]) for b in range(4)]
            return parts

        def finish(parts):
            highest = max_of(parts)
            augs = [aug_scr[side * 4 + b] for b in range(4)]
            if odd:
                augs += [aug_scr[(1 - side) * 4 + b] for b in range(4)]
            mixed = weigh(parts, highest, augs)
            acc_ref[side, h] = mixed[:, :HD]
            old = jnp.where(lane == h, highest, stat_ref[side])
            stat_ref[side] = jnp.where(lane == h + 8, mixed[:, HD:], old)

        return score, finish

    in_turn([step(odd, h) for odd in (True, False) for h in range(GROUP)])


def last_kernel(own, q_ref, acc_ref, stat_ref, *refs):
    kv_refs = refs[:4]
    out_ref, extra_ref, aug_scr, out_scr, sems = refs[-5:]
    if own:
        extra_ref[...] = jnp.zeros_like(extra_ref)
    else:
        extra_ref[0] = refs[4][...]
        extra_ref[1] = refs[5][...]
    z, _, parity = place()
    side = 0 if own else 1
    if own:
        q_ref = q_ref.at[parity]
        out_ref = out_ref.at[parity]
    lane = lax.broadcasted_iota(jnp.int32, (BLOCK, HD), 1)

    def column(h):
        return stat_ref[side, :, h : h + 1]

    def copy_of(half):
        at = slice(half * 4 * HD, (half + 1) * 4 * HD)
        return pltpu.make_async_copy(out_scr.at[:, at], out_ref.at[:, at], sems.at[half])

    def store(h, rows):
        out_scr[:, h * HD : (h + 1) * HD] = rows.astype(bf16)
        if h % 4 == 3:
            copy_of(h // 4).start()

    @pl.when(z >= 2)
    def _():
        for b in range(8):
            fill_values(aug_scr, b, kv_refs[b // 2][b % 2])

        def step(h):
            def score():
                rows = q_ref[:, h * HD : (h + 1) * HD]
                return [scores_of(rows, kv_refs[b // 2][b % 2, :, :HD]) for b in range(8)]

            def finish(parts):
                before = column(h)
                highest = jnp.maximum(before, max_of(parts))
                mixed = weigh(parts, highest, [aug_scr[b] for b in range(8)])
                fade = jnp.exp2((before - highest) * SCALE2)
                total = column(h + 8) * fade + mixed[:, HD:]
                store(h, (acc_ref[side, h] * fade + mixed[:, :HD]) / total)

            return score, finish

        in_turn([step(h) for h in range(GROUP)])

    @pl.when(z < 2)
    def _():
        for h in range(GROUP):
            store(h, acc_ref[side, h] / column(h + 8))

    for half in range(2):
        copy_of(half).wait()


def segment_kernel(prompt_ref, _, rows0_ref, rows1_ref, *refs):
    kv_refs = refs[:8]
    out0_ref, out1_ref, done_ref, aug_scr = refs[-4:]
    done_ref[...] = jnp.zeros_like(done_ref)
    index, pool = lax.axis_index("ctx"), lax.axis_index("pd")
    parity = place()[2]

    def block_of(b, at):
        return kv_refs[b // 2][b % 2, :, at]

    for b in range(16):
        aug_scr[b, :, :HD] = block_of(b, slice(HD, 2 * HD))
        aug_scr[b, :, HD:] = jnp.ones((BLOCK, HD), bf16)
    lane = lax.broadcasted_iota(jnp.int32, (DECODE_ROWS, HD), 1)

    for which, rows_ref, out_ref in ((0, rows0_ref, out0_ref), (1, rows1_ref, out1_ref)):
        needed = prompt_ref[pool, index ^ (4 * which)] == parity

        @pl.when(needed)
        def _():
            stats = [jnp.zeros((DECODE_ROWS, HD), f32)]
            state = {}

            def step(tile, chunk):
                heads = range(tile * 4, tile * 4 + 4)
                blocks = range(chunk * 8, chunk * 8 + 8)

                def score():
                    rows = jnp.concatenate(
                        [rows_ref[:, h * HD : (h + 1) * HD] for h in heads], axis=0
                    )
                    return [scores_of(rows, block_of(b, slice(0, HD))) for b in blocks]

                def finish(parts):
                    top = max_of(parts)
                    augs = [aug_scr[b] for b in blocks]
                    if chunk == 0:
                        state[tile] = (top, weigh(parts, top, augs))
                        return
                    highest, mixed = state[tile]
                    top = jnp.maximum(top, highest)
                    mixed = mixed * jnp.exp2((highest - top) * SCALE2) + weigh(parts, top, augs)
                    total = mixed[:, HD:]
                    share = (mixed[:, :HD] / total).astype(bf16)
                    level = top * SCALE2 + jnp.log2(total)
                    for i, h in enumerate(heads):
                        at = slice(i * DECODE_ROWS, (i + 1) * DECODE_ROWS)
                        out_ref[:, h * HD : (h + 1) * HD] = share[at]
                        stats[0] = jnp.where(lane == h, level[at], stats[0])

                return score, finish

            in_turn([step(tile, chunk) for tile in range(2) for chunk in range(2)])
            stat = stats[0]
            high = stat.astype(bf16).astype(f32)
            middle = (stat - high).astype(bf16).astype(f32)
            low = stat - high - middle
            pieces = high + pltpu.roll(middle, 8, 1) + pltpu.roll(low, 16, 1)
            out_ref[:, GROUP * HD :] = pieces.astype(bf16)

        @pl.when(jnp.logical_not(needed))
        def _():
            out_ref[...] = jnp.zeros_like(out_ref)


def local_kernel(
    len_ref, _, cos_ref, sin_ref, gain_ref, q_ref, own_ref, twin_ref, *refs
):
    pairs = refs[:3]
    weight_ref, cache_ref = refs[3:5]
    out_ref, level_ref = refs[-2:]
    width = own_ref.shape[1]
    core, x = lax.axis_index("tp") % 2, lax.axis_index("tp") // 2
    ones = jnp.ones((BLOCK, HD), bf16)
    row = lax.broadcasted_iota(jnp.int32, (128, BLOCK), 0)
    slot = lax.broadcasted_iota(jnp.int32, (128, BLOCK), 1)
    fresh_row = lax.broadcasted_iota(jnp.int32, (128, DECODE_ROWS), 0) % 16
    fresh_slot = lax.broadcasted_iota(jnp.int32, (128, DECODE_ROWS), 1)

    groups = []
    for g in range(4):
        rows = jnp.concatenate(
            [q_ref[g * 16 : g * 16 + 16, h * HD : (h + 1) * HD] for h in range(GROUP)], axis=0
        )
        parts = []
        for j in range(4):
            s = g * 4 + j
            allowed = (row % 16 // 4 == j) & (slot < len_ref[s])
            parts.append(jnp.where(allowed, scores_of(rows, cache_ref[s, :, :HD]), MASKED))
        groups.append((rows, parts))

    squares = jnp.zeros((DECODE_ROWS, 1), f32)
    projected = jnp.zeros((DECODE_ROWS, 2 * HD), f32)
    for i, step in enumerate((0, 3, 1, 2)):
        for side in range(2):
            owner = ((x + step) % 4) * 2 + (core if side == 0 else 1 - core)
            if i == 0:
                wide = (own_ref, twin_ref)[side][...].astype(f32)
            else:
                wide = pairs[i - 1][side].astype(f32)
            at = pl.ds(pl.multiple_of(owner * width, width), width)
            squares = squares + jnp.sum(wide * wide, axis=-1, keepdims=True)
            scaled = (wide * gain_ref[:, at]).astype(bf16)
            projected = projected + jnp.dot(
                scaled, weight_ref[at], preferred_element_type=f32
            )
    normed = projected * lax.rsqrt(squares / D + 1e-6)
    key_rows = normed[:, :HD]
    turned = pltpu.roll(key_rows, HD // 2, 1)
    fresh_k = (key_rows * cos_ref[...] + turned * sin_ref[...]).astype(bf16)
    fresh_v = normed[:, HD:].astype(bf16)
    fresh_aug = jnp.concatenate([fresh_v, jnp.ones((DECODE_ROWS, HD), bf16)], axis=1)

    for g, (rows, parts) in enumerate(groups):
        at = slice(g * 16, (g + 1) * 16)
        augs = [
            jnp.concatenate([cache_ref[g * 4 + j, :, HD:], ones], axis=1) for j in range(4)
        ]
        behind = fresh_row + g * 16 - fresh_slot
        allowed = (behind >= 0) & (behind <= fresh_row % 4)
        fresh_part = jnp.where(allowed, scores_of(rows, fresh_k), MASKED)
        highest = jnp.maximum(max_of(parts), jnp.max(fresh_part, axis=-1, keepdims=True))
        mixed = weigh(parts + [fresh_part], highest, augs + [fresh_aug])
        total = mixed[:, HD:]
        share = mixed[:, :HD] / total
        level = highest * SCALE2 + jnp.log2(total)
        for h in range(GROUP):
            out_ref[at, h * HD : (h + 1) * HD] = share[h * 16 : (h + 1) * 16]
            level_ref[at, h * HD : (h + 1) * HD] = level[h * 16 : (h + 1) * 16]


def merge_kernel(
    prompt_ref, local_ref, level_ref, same_ref, other_ref, returned_ref, own_out, out_ref, full_ref,
    sem,
):
    del own_out
    parity = place()[2]
    copy = pltpu.make_async_copy(returned_ref, full_ref.at[1 - parity], sem)
    copy.start()
    lane = lax.broadcasted_iota(jnp.int32, (DECODE_ROWS, HD), 1)
    held_here = prompt_ref[1 - lax.axis_index("pd"), lax.axis_index("ctx")] == parity

    def merge(part_ref):
        pieces = part_ref[:, GROUP * HD :].astype(f32)
        for h in range(GROUP):
            at = slice(h * HD, (h + 1) * HD)
            mine = (lane == h) | (lane == h + 8) | (lane == h + 16)
            far = jnp.sum(jnp.where(mine, pieces, 0.0), axis=-1, keepdims=True)
            near = level_ref[:, at]
            top = jnp.maximum(far, near)
            far_share = jnp.exp2(far - top)
            near_share = jnp.exp2(near - top)
            mixed = part_ref[:, at].astype(f32) * far_share + local_ref[:, at] * near_share
            merged = mixed / (far_share + near_share)
            for s in range(16):
                out_ref[s, :, at] = merged[s * 4 : s * 4 + 4].astype(bf16)

    @pl.when(held_here)
    def _():
        merge(same_ref)

    @pl.when(jnp.logical_not(held_here))
    def _():
        merge(other_ref)

    copy.wait()


SMEM = pl.BlockSpec(memory_space=pltpu.SMEM)
VMEM = pl.BlockSpec(memory_space=pltpu.VMEM)
ANY = pl.BlockSpec(memory_space=pl.ANY)


def call(
    kernel, out_shape, args, scalars=0, scratch=(), flops=0, touched=0, exps=0, specs=None,
    out_specs=None, aliases=None, vmem=14,
):
    in_specs = [SMEM] * scalars + [VMEM] * (len(args) - scalars)
    for at, spec in (specs or {}).items():
        in_specs[at] = spec
    return pl.pallas_call(
        kernel,
        out_shape=out_shape,
        in_specs=in_specs,
        out_specs=out_specs or jax.tree.map(lambda _: VMEM, out_shape),
        scratch_shapes=list(scratch),
        input_output_aliases=aliases or {},
        compiler_params=pltpu.CompilerParams(vmem_limit_bytes=vmem * MIB),
        cost_estimate=pl.CostEstimate(flops=flops, bytes_accessed=touched, transcendentals=exps),
    )(*args)


def after(value, *others):
    return lax.optimization_barrier((value, *others))[0]


def y_turn(block, distance):
    route = [(i, i // 4 * 4 + (i % 4 + distance) % 4) for i in range(16)]
    return lax.ppermute(block, "ctx", route)


def z_swap(block, bits):
    return lax.ppermute(block, "ctx", [(i, i ^ (4 * bits)) for i in range(16)])


def y_all(block):
    return [block, y_turn(block, 1), y_turn(block, -1), y_turn(block, 2)]


def tp_turn(block, distance):
    return lax.ppermute(block, "tp", [(i, (i + distance) % 8) for i in range(8)])


def pool_swap(block, z_bits):
    route = [(i, (i ^ 1) ^ (8 * z_bits)) for i in range(32)]
    return lax.ppermute(block, ("ctx", "pd"), route)


def on_device(
    prefill_query,
    prefill_kv,
    decode_query,
    gen_cache,
    new_hidden,
    norm_gain,
    kv_weight,
    prompt_of,
    cached_len,
):
    queries = prefill_query[0]
    keyvals = prefill_kv[0]
    even = lax.axis_index("ctx") // 4 % 2 == 0
    shape = jax.ShapeDtypeStruct

    kv_keep = jnp.where(even, keyvals[0], keyvals[1])
    kv_give = jnp.where(even, keyvals[1], keyvals[0])
    from_z1 = z_swap(kv_give, 1)
    from_z2 = z_swap(kv_keep, 2)
    from_z3 = z_swap(kv_give, 3)
    q_give = lax.dynamic_index_in_dim(queries, even.astype(jnp.int32), 0, keepdims=False)
    samples, steps, width = new_hidden.shape[2:]
    decode_rows = samples * steps
    from_z1, q_give = lax.optimization_barrier((from_z1, q_give))
    first_pair, q_give = lax.optimization_barrier((jnp.stack([kv_keep, from_z1]), q_give))
    group01 = y_all(first_pair)
    q_partner = z_swap(q_give, 1)
    group23 = y_all(jnp.stack([from_z2, from_z3]))

    lengths = cached_len[0, 0]
    half = HD // 2
    frequency = 1000000.0 ** (-jnp.arange(half, dtype=f32) * 2.0 / HD)
    positions = (4096 + lengths[:, None] + jnp.arange(steps, dtype=jnp.int32)[None, :]).astype(f32)
    angles = positions.reshape(-1)[:, None] * frequency
    cosine, sine = jnp.cos(angles), jnp.sin(angles)
    cos_all = jnp.concatenate([cosine, cosine], axis=-1)
    sin_all = jnp.concatenate([-sine, sine], axis=-1)

    token = shape((8, HD), f32)
    flat = shape((decode_rows, width), bf16)
    acc, stat, hidden, step_rows = call(
        first_kernel,
        (shape((2, GROUP, BLOCK, HD), f32), shape((2, BLOCK, HD), f32), flat, flat),
        (queries, q_partner, new_hidden[0, 0], decode_query[0, 0], *group01),
        scratch=(
            pltpu.VMEM((8, BLOCK, 2 * HD), bf16),
        ),
        flops=3 * 2048 * 1024 * 512,
        touched=4 << 20,
        exps=3 * 2048 * 1024,
    )
    twin = lax.ppermute(hidden, "tp", [(i, i ^ 1) for i in range(8)])
    rows_pair = [pool_swap(step_rows, 0), pool_swap(step_rows, 1)]

    def finish(own, q_rows, extra):
        out_rows = (BLOCK, GROUP * HD)
        last = token if own else shape((2, decode_rows, width), bf16)
        return call(
            functools.partial(last_kernel, own),
            (shape((2, *out_rows) if own else out_rows, bf16), last),
            (q_rows, acc, stat, *group23, *extra),
            scratch=(
                pltpu.VMEM((8, BLOCK, 2 * HD), bf16),
                pltpu.VMEM(out_rows, bf16),
                pltpu.SemaphoreType.DMA((2,)),
            ),
            specs={7: ANY} if own else None,
            out_specs=(ANY, VMEM),
            flops=2 * 2048 * 1024 * 512,
            touched=4 << 20,
            exps=2 * 2048 * 1024,
        )

    out_partner, pair = finish(False, q_partner, (hidden, twin))
    returned = z_swap(out_partner, 1)
    pairs = [tp_turn(pair, 2), tp_turn(pair, -2), tp_turn(pair, 4)]
    part = shape((decode_rows, width + HD), bf16)
    segment0, segment1, segment_done = call(
        segment_kernel,
        (part, part, token),
        (prompt_of, pair, *rows_pair, *group01, *group23),
        specs={1: ANY},
        scalars=1,
        scratch=(pltpu.VMEM((16, BLOCK, 2 * HD), bf16),),
        flops=1024 * 4096 * 512,
        touched=3 << 20,
        exps=1024 * 4096,
    )
    back0 = pool_swap(segment0, 0)
    back1 = pool_swap(segment1, 1)
    out_own, own_done = finish(True, queries, (segment_done,))
    local_out, local_level = call(
        local_kernel,
        (shape((decode_rows, width), f32), shape((decode_rows, width), f32)),
        (
            lengths,
            own_done,
            cos_all,
            sin_all,
            norm_gain[None],
            step_rows,
            hidden,
            twin,
            *pairs,
            kv_weight,
            gen_cache[0, 0],
        ),
        scalars=1,
        specs={1: ANY},
        flops=2 * 64 * D * 256,
        touched=8 << 20,
        exps=512 * 320,
    )

    merged, segment_out = call(
        merge_kernel,
        (shape((samples, steps, width), bf16), shape(queries.shape, bf16)),
        (prompt_of, local_out, local_level, back0, back1, returned, out_own),
        scalars=1,
        scratch=(pltpu.SemaphoreType.DMA,),
        flops=512 * HD * 8,
        touched=1 << 20,
        exps=512 * HD * 2,
        specs={5: ANY, 6: ANY},
        out_specs=(VMEM, ANY),
        aliases={6: 1},
        vmem=8,
    )
    return (segment_out[None], merged[None, None])


def solution(mesh):
    placed = (
        P("pd", None, "ctx", "tp"),
        P("pd", None, "ctx", "tp"),
        P("pd", "ctx", None, None, "tp"),
        P("pd", "ctx", None, None, "tp"),
        P("pd", "ctx", None, None, "tp"),
        P(),
        P(None, "tp"),
        P(),
        P("pd", "ctx", None),
    )
    return jax.shard_map(
        on_device,
        mesh=mesh,
        in_specs=placed,
        out_specs=(P("pd", None, "ctx", "tp"), P("pd", "ctx", None, None, "tp")),
        check_vma=False,
    )
```

```python
import functools

import jax
import jax.numpy as jnp
from jax import lax
from jax.experimental import pallas as pl
from jax.experimental.pallas import tpu as pltpu
from jax.sharding import PartitionSpec as P

D = 8192
HD = 128
GROUP = 8
BLOCK = 256
DECODE_ROWS = 64
MASKED = -1e30
LOG2E = 1.4426950408889634
SCALE2 = HD ** (-0.5) * LOG2E
MIB = 1024 * 1024

bf16 = jnp.bfloat16
f32 = jnp.float32


def scores_of(rows, keys):
    return lax.dot_general(rows, keys, (((1,), (1,)), ((), ())), preferred_element_type=f32)


def place():
    index = lax.axis_index("ctx")
    return index // 4, index % 4, index // 4 % 2


def fill_values(aug_ref, index, block):
    aug_ref[index, :, :HD] = block[:, HD:]
    aug_ref[index, :, HD:] = jnp.ones((BLOCK, HD), bf16)


def weigh(parts, highest, aug_blocks):
    out = None
    for part, aug in zip(parts, aug_blocks):
        weights = jnp.exp2((part - highest) * SCALE2).astype(bf16)
        term = jnp.dot(weights, aug, preferred_element_type=f32)
        out = term if out is None else out + term
    return out


def max_of(parts):
    top = parts[0]
    for part in parts[1:]:
        top = jnp.maximum(top, part)
    return jnp.max(top, axis=-1, keepdims=True)


def in_turn(steps):
    parts = steps[0][0]()
    for i, (_, finish) in enumerate(steps):
        following = steps[i + 1][0]() if i + 1 < len(steps) else None
        finish(parts)
        parts = following


def flatten(target_ref, source_ref):
    for s in range(16):
        target_ref[s * 4 : s * 4 + 4] = source_ref[s]


def first_kernel(own_q, partner_q, hidden_in, rows_in, *refs):
    blocks = refs[:4]
    acc_ref, stat_ref, hidden_ref, rows_ref, aug_scr = refs[4:]
    flatten(hidden_ref, hidden_in)
    flatten(rows_ref, rows_in)
    _, row_y, parity = place()
    for group in range(2):
        for b in range(4):
            fill_values(aug_scr, group * 4 + b, blocks[b][group])
    lane = lax.broadcasted_iota(jnp.int32, (BLOCK, HD), 1)
    upper = lax.broadcasted_iota(jnp.int32, (BLOCK, BLOCK), 1) > lax.broadcasted_iota(
        jnp.int32, (BLOCK, BLOCK), 0
    )

    def shift_of(b):
        block_y = (row_y + (0, 3, 1, 2)[b]) % 4
        return jnp.where(block_y < row_y, 0.0, MASKED).astype(f32)

    def step(odd, h):
        side = 1 - parity if odd else parity
        at = pl.ds(pl.multiple_of(h * HD, HD), HD)

        def score():
            rows = jnp.where(side == 0, own_q[parity, :, at], partner_q[:, at])
            parts = []
            for b in range(4):
                part = scores_of(rows, blocks[b][side, :, :HD])
                if b == 0:
                    parts.append(jnp.where(upper, MASKED, part))
                else:
                    parts.append(part + shift_of(b))
            if odd:
                parts += [scores_of(rows, blocks[b][1 - side, :, :HD]) for b in range(4)]
            return parts

        def finish(parts):
            highest = max_of(parts)
            augs = [aug_scr[side * 4 + b] for b in range(4)]
            if odd:
                augs += [aug_scr[(1 - side) * 4 + b] for b in range(4)]
            mixed = weigh(parts, highest, augs)
            acc_ref[side, h] = mixed[:, :HD]
            old = jnp.where(lane == h, highest, stat_ref[side])
            stat_ref[side] = jnp.where(lane == h + 8, mixed[:, HD:], old)

        return score, finish

    for odd in (True, False):

        def four(half, carry, odd=odd):
            in_turn([step(odd, half * 4 + i) for i in range(4)])
            return carry

        lax.fori_loop(0, 2, four, 0)


def last_kernel(own, q_ref, acc_ref, stat_ref, *refs):
    kv_refs = refs[:4]
    out_ref, extra_ref, aug_scr, out_scr, sems = refs[-5:]
    if own:
        extra_ref[...] = jnp.zeros_like(extra_ref)
    else:
        extra_ref[0] = refs[4][...]
        extra_ref[1] = refs[5][...]
    z, _, parity = place()
    side = 0 if own else 1
    if own:
        q_ref = q_ref.at[parity]
        out_ref = out_ref.at[parity]
    lane = lax.broadcasted_iota(jnp.int32, (BLOCK, HD), 1)

    def column(h):
        return jnp.sum(jnp.where(lane == h, stat_ref[side], 0.0), axis=-1, keepdims=True)

    def head_at(h):
        return pl.ds(pl.multiple_of(h * HD, HD), HD)

    def copy_of(half):
        at = pl.ds(pl.multiple_of(half * 4 * HD, 4 * HD), 4 * HD)
        return pltpu.make_async_copy(out_scr.at[:, at], out_ref.at[:, at], sems.at[half])

    @pl.when(z >= 2)
    def _():
        for b in range(8):
            fill_values(aug_scr, b, kv_refs[b // 2][b % 2])

        def step(h):
            def score():
                rows = q_ref[:, head_at(h)]
                return [scores_of(rows, kv_refs[b // 2][b % 2, :, :HD]) for b in range(8)]

            def finish(parts):
                before = column(h)
                highest = jnp.maximum(before, max_of(parts))
                mixed = weigh(parts, highest, [aug_scr[b] for b in range(8)])
                fade = jnp.exp2((before - highest) * SCALE2)
                total = column(h + 8) * fade + mixed[:, HD:]
                rows = (acc_ref[side, h] * fade + mixed[:, :HD]) / total
                out_scr[:, head_at(h)] = rows.astype(bf16)

            return score, finish

        def four(half, carry):
            in_turn([step(half * 4 + i) for i in range(4)])
            copy_of(half).start()
            return carry

        lax.fori_loop(0, 2, four, 0)

    @pl.when(z < 2)
    def _():
        def four(half, carry):
            for i in range(4):
                h = half * 4 + i
                out_scr[:, head_at(h)] = (acc_ref[side, h] / column(h + 8)).astype(bf16)
            copy_of(half).start()
            return carry

        lax.fori_loop(0, 2, four, 0)

    for half in range(2):
        copy_of(half).wait()


def segment_kernel(prompt_ref, _, rows0_ref, rows1_ref, *refs):
    kv_refs = refs[:8]
    out0_ref, out1_ref, done_ref, aug_scr = refs[-4:]
    done_ref[...] = jnp.zeros_like(done_ref)
    index, pool = lax.axis_index("ctx"), lax.axis_index("pd")
    parity = place()[2]

    def block_of(b, at):
        return kv_refs[b // 2][b % 2, :, at]

    for b in range(16):
        aug_scr[b, :, :HD] = block_of(b, slice(HD, 2 * HD))
        aug_scr[b, :, HD:] = jnp.ones((BLOCK, HD), bf16)
    lane = lax.broadcasted_iota(jnp.int32, (DECODE_ROWS, HD), 1)

    for which, rows_ref, out_ref in ((0, rows0_ref, out0_ref), (1, rows1_ref, out1_ref)):
        needed = prompt_ref[pool, index ^ (4 * which)] == parity

        @pl.when(needed)
        def _():
            stats = [jnp.zeros((DECODE_ROWS, HD), f32)]
            state = {}

            def step(tile, chunk):
                heads = range(tile * 4, tile * 4 + 4)
                blocks = range(chunk * 8, chunk * 8 + 8)

                def score():
                    rows = jnp.concatenate(
                        [rows_ref[:, h * HD : (h + 1) * HD] for h in heads], axis=0
                    )
                    return [scores_of(rows, block_of(b, slice(0, HD))) for b in blocks]

                def finish(parts):
                    top = max_of(parts)
                    augs = [aug_scr[b] for b in blocks]
                    if chunk == 0:
                        state[tile] = (top, weigh(parts, top, augs))
                        return
                    highest, mixed = state[tile]
                    top = jnp.maximum(top, highest)
                    mixed = mixed * jnp.exp2((highest - top) * SCALE2) + weigh(parts, top, augs)
                    total = mixed[:, HD:]
                    share = (mixed[:, :HD] / total).astype(bf16)
                    level = top * SCALE2 + jnp.log2(total)
                    for i, h in enumerate(heads):
                        at = slice(i * DECODE_ROWS, (i + 1) * DECODE_ROWS)
                        out_ref[:, h * HD : (h + 1) * HD] = share[at]
                        stats[0] = jnp.where(lane == h, level[at], stats[0])

                return score, finish

            in_turn([step(tile, chunk) for tile in range(2) for chunk in range(2)])
            stat = stats[0]
            high = stat.astype(bf16).astype(f32)
            middle = (stat - high).astype(bf16).astype(f32)
            low = stat - high - middle
            pieces = high + pltpu.roll(middle, 8, 1) + pltpu.roll(low, 16, 1)
            out_ref[:, GROUP * HD :] = pieces.astype(bf16)

        @pl.when(jnp.logical_not(needed))
        def _():
            out_ref[...] = jnp.zeros_like(out_ref)


def local_kernel(
    len_ref, _, cos_ref, sin_ref, gain_ref, q_ref, own_ref, twin_ref, *refs
):
    pairs = refs[:3]
    weight_ref, cache_ref = refs[3:5]
    out_ref, level_ref = refs[-2:]
    width = own_ref.shape[1]
    core, x = lax.axis_index("tp") % 2, lax.axis_index("tp") // 2
    ones = jnp.ones((BLOCK, HD), bf16)
    row = lax.broadcasted_iota(jnp.int32, (128, BLOCK), 0)
    slot = lax.broadcasted_iota(jnp.int32, (128, BLOCK), 1)
    fresh_row = lax.broadcasted_iota(jnp.int32, (128, DECODE_ROWS), 0) % 16
    fresh_slot = lax.broadcasted_iota(jnp.int32, (128, DECODE_ROWS), 1)

    groups = []
    for g in range(4):
        rows = jnp.concatenate(
            [q_ref[g * 16 : g * 16 + 16, h * HD : (h + 1) * HD] for h in range(GROUP)], axis=0
        )
        parts = []
        for j in range(4):
            s = g * 4 + j
            allowed = (row % 16 // 4 == j) & (slot < len_ref[s])
            parts.append(jnp.where(allowed, scores_of(rows, cache_ref[s, :, :HD]), MASKED))
        groups.append((rows, parts))

    squares = jnp.zeros((DECODE_ROWS, 1), f32)
    projected = jnp.zeros((DECODE_ROWS, 2 * HD), f32)
    for i, step in enumerate((0, 3, 1, 2)):
        for side in range(2):
            owner = ((x + step) % 4) * 2 + (core if side == 0 else 1 - core)
            if i == 0:
                wide = (own_ref, twin_ref)[side][...].astype(f32)
            else:
                wide = pairs[i - 1][side].astype(f32)
            at = pl.ds(pl.multiple_of(owner * width, width), width)
            squares = squares + jnp.sum(wide * wide, axis=-1, keepdims=True)
            scaled = (wide * gain_ref[:, at]).astype(bf16)
            projected = projected + jnp.dot(
                scaled, weight_ref[at], preferred_element_type=f32
            )
    normed = projected * lax.rsqrt(squares / D + 1e-6)
    key_rows = normed[:, :HD]
    turned = pltpu.roll(key_rows, HD // 2, 1)
    fresh_k = (key_rows * cos_ref[...] + turned * sin_ref[...]).astype(bf16)
    fresh_v = normed[:, HD:].astype(bf16)
    fresh_aug = jnp.concatenate([fresh_v, jnp.ones((DECODE_ROWS, HD), bf16)], axis=1)

    for g, (rows, parts) in enumerate(groups):
        at = slice(g * 16, (g + 1) * 16)
        augs = [
            jnp.concatenate([cache_ref[g * 4 + j, :, HD:], ones], axis=1) for j in range(4)
        ]
        behind = fresh_row + g * 16 - fresh_slot
        allowed = (behind >= 0) & (behind <= fresh_row % 4)
        fresh_part = jnp.where(allowed, scores_of(rows, fresh_k), MASKED)
        highest = jnp.maximum(max_of(parts), jnp.max(fresh_part, axis=-1, keepdims=True))
        mixed = weigh(parts + [fresh_part], highest, augs + [fresh_aug])
        total = mixed[:, HD:]
        share = mixed[:, :HD] / total
        level = highest * SCALE2 + jnp.log2(total)
        for h in range(GROUP):
            out_ref[at, h * HD : (h + 1) * HD] = share[h * 16 : (h + 1) * 16]
            level_ref[at, h * HD : (h + 1) * HD] = level[h * 16 : (h + 1) * 16]


def merge_kernel(
    prompt_ref, local_ref, level_ref, same_ref, other_ref, returned_ref, own_out, out_ref, full_ref,
    sem,
):
    del own_out
    parity = place()[2]
    copy = pltpu.make_async_copy(returned_ref, full_ref.at[1 - parity], sem)
    copy.start()
    lane = lax.broadcasted_iota(jnp.int32, (DECODE_ROWS, HD), 1)
    held_here = prompt_ref[1 - lax.axis_index("pd"), lax.axis_index("ctx")] == parity

    def merge(part_ref):
        pieces = part_ref[:, GROUP * HD :].astype(f32)
        for h in range(GROUP):
            at = slice(h * HD, (h + 1) * HD)
            mine = (lane == h) | (lane == h + 8) | (lane == h + 16)
            far = jnp.sum(jnp.where(mine, pieces, 0.0), axis=-1, keepdims=True)
            near = level_ref[:, at]
            top = jnp.maximum(far, near)
            far_share = jnp.exp2(far - top)
            near_share = jnp.exp2(near - top)
            mixed = part_ref[:, at].astype(f32) * far_share + local_ref[:, at] * near_share
            merged = mixed / (far_share + near_share)
            for s in range(16):
                out_ref[s, :, at] = merged[s * 4 : s * 4 + 4].astype(bf16)

    @pl.when(held_here)
    def _():
        merge(same_ref)

    @pl.when(jnp.logical_not(held_here))
    def _():
        merge(other_ref)

    copy.wait()


SMEM = pl.BlockSpec(memory_space=pltpu.SMEM)
VMEM = pl.BlockSpec(memory_space=pltpu.VMEM)
ANY = pl.BlockSpec(memory_space=pl.ANY)


def call(
    kernel, out_shape, args, scalars=0, scratch=(), flops=0, touched=0, exps=0, specs=None,
    out_specs=None, aliases=None, vmem=14,
):
    in_specs = [SMEM] * scalars + [VMEM] * (len(args) - scalars)
    for at, spec in (specs or {}).items():
        in_specs[at] = spec
    return pl.pallas_call(
        kernel,
        out_shape=out_shape,
        in_specs=in_specs,
        out_specs=out_specs or jax.tree.map(lambda _: VMEM, out_shape),
        scratch_shapes=list(scratch),
        input_output_aliases=aliases or {},
        compiler_params=pltpu.CompilerParams(vmem_limit_bytes=vmem * MIB),
        cost_estimate=pl.CostEstimate(flops=flops, bytes_accessed=touched, transcendentals=exps),
    )(*args)


def after(value, *others):
    return lax.optimization_barrier((value, *others))[0]


def y_turn(block, distance):
    route = [(i, i // 4 * 4 + (i % 4 + distance) % 4) for i in range(16)]
    return lax.ppermute(block, "ctx", route)


def z_swap(block, bits):
    return lax.ppermute(block, "ctx", [(i, i ^ (4 * bits)) for i in range(16)])


def y_all(block):
    return [block, y_turn(block, 1), y_turn(block, -1), y_turn(block, 2)]


def tp_turn(block, distance):
    return lax.ppermute(block, "tp", [(i, (i + distance) % 8) for i in range(8)])


def pool_swap(block, z_bits):
    route = [(i, (i ^ 1) ^ (8 * z_bits)) for i in range(32)]
    return lax.ppermute(block, ("ctx", "pd"), route)


def on_device(
    prefill_query,
    prefill_kv,
    decode_query,
    gen_cache,
    new_hidden,
    norm_gain,
    kv_weight,
    prompt_of,
    cached_len,
):
    queries = prefill_query[0]
    keyvals = prefill_kv[0]
    even = lax.axis_index("ctx") // 4 % 2 == 0
    shape = jax.ShapeDtypeStruct

    kv_keep = jnp.where(even, keyvals[0], keyvals[1])
    kv_give = jnp.where(even, keyvals[1], keyvals[0])
    from_z1 = z_swap(kv_give, 1)
    from_z2 = z_swap(kv_keep, 2)
    from_z3 = z_swap(kv_give, 3)
    q_give = lax.dynamic_index_in_dim(queries, even.astype(jnp.int32), 0, keepdims=False)
    samples, steps, width = new_hidden.shape[2:]
    decode_rows = samples * steps
    from_z1, q_give = lax.optimization_barrier((from_z1, q_give))
    first_pair, q_give = lax.optimization_barrier((jnp.stack([kv_keep, from_z1]), q_give))
    group01 = y_all(first_pair)
    q_partner = z_swap(q_give, 1)
    group23 = y_all(jnp.stack([from_z2, from_z3]))

    lengths = cached_len[0, 0]
    half = HD // 2
    frequency = 1000000.0 ** (-jnp.arange(half, dtype=f32) * 2.0 / HD)
    positions = (4096 + lengths[:, None] + jnp.arange(steps, dtype=jnp.int32)[None, :]).astype(f32)
    angles = positions.reshape(-1)[:, None] * frequency
    cosine, sine = jnp.cos(angles), jnp.sin(angles)
    cos_all = jnp.concatenate([cosine, cosine], axis=-1)
    sin_all = jnp.concatenate([-sine, sine], axis=-1)

    token = shape((8, HD), f32)
    flat = shape((decode_rows, width), bf16)
    acc, stat, hidden, step_rows = call(
        first_kernel,
        (shape((2, GROUP, BLOCK, HD), f32), shape((2, BLOCK, HD), f32), flat, flat),
        (queries, q_partner, new_hidden[0, 0], decode_query[0, 0], *group01),
        scratch=(
            pltpu.VMEM((8, BLOCK, 2 * HD), bf16),
        ),
        flops=3 * 2048 * 1024 * 512,
        touched=4 << 20,
        exps=3 * 2048 * 1024,
    )
    twin = lax.ppermute(hidden, "tp", [(i, i ^ 1) for i in range(8)])
    rows_pair = [pool_swap(step_rows, 0), pool_swap(step_rows, 1)]

    def finish(own, q_rows, extra):
        out_rows = (BLOCK, GROUP * HD)
        last = token if own else shape((2, decode_rows, width), bf16)
        return call(
            functools.partial(last_kernel, own),
            (shape((2, *out_rows) if own else out_rows, bf16), last),
            (q_rows, acc, stat, *group23, *extra),
            scratch=(
                pltpu.VMEM((8, BLOCK, 2 * HD), bf16),
                pltpu.VMEM(out_rows, bf16),
                pltpu.SemaphoreType.DMA((2,)),
            ),
            specs={7: ANY} if own else None,
            out_specs=(ANY, VMEM),
            flops=2 * 2048 * 1024 * 512,
            touched=4 << 20,
            exps=2 * 2048 * 1024,
        )

    out_partner, pair = finish(False, q_partner, (hidden, twin))
    returned = z_swap(out_partner, 1)
    pairs = [tp_turn(pair, 2), tp_turn(pair, -2), tp_turn(pair, 4)]
    part = shape((decode_rows, width + HD), bf16)
    segment0, segment1, segment_done = call(
        segment_kernel,
        (part, part, token),
        (prompt_of, pair, *rows_pair, *group01, *group23),
        specs={1: ANY},
        scalars=1,
        scratch=(pltpu.VMEM((16, BLOCK, 2 * HD), bf16),),
        flops=1024 * 4096 * 512,
        touched=3 << 20,
        exps=1024 * 4096,
    )
    back0 = pool_swap(segment0, 0)
    back1 = pool_swap(segment1, 1)
    out_own, own_done = finish(True, queries, (segment_done,))
    local_out, local_level = call(
        local_kernel,
        (shape((decode_rows, width), f32), shape((decode_rows, width), f32)),
        (
            lengths,
            own_done,
            cos_all,
            sin_all,
            norm_gain[None],
            step_rows,
            hidden,
            twin,
            *pairs,
            kv_weight,
            gen_cache[0, 0],
        ),
        scalars=1,
        specs={1: ANY},
        flops=2 * 64 * D * 256,
        touched=8 << 20,
        exps=512 * 320,
    )

    merged, segment_out = call(
        merge_kernel,
        (shape((samples, steps, width), bf16), shape(queries.shape, bf16)),
        (prompt_of, local_out, local_level, back0, back1, returned, out_own),
        scalars=1,
        scratch=(pltpu.SemaphoreType.DMA,),
        flops=512 * HD * 8,
        touched=1 << 20,
        exps=512 * HD * 2,
        specs={5: ANY, 6: ANY},
        out_specs=(VMEM, ANY),
        aliases={6: 1},
        vmem=8,
    )
    return (segment_out[None], merged[None, None])


def solution(mesh):
    placed = (
        P("pd", None, "ctx", "tp"),
        P("pd", None, "ctx", "tp"),
        P("pd", "ctx", None, None, "tp"),
        P("pd", "ctx", None, None, "tp"),
        P("pd", "ctx", None, None, "tp"),
        P(),
        P(None, "tp"),
        P(),
        P("pd", "ctx", None),
    )
    return jax.shard_map(
        on_device,
        mesh=mesh,
        in_specs=placed,
        out_specs=(P("pd", None, "ctx", "tp"), P("pd", "ctx", None, None, "tp")),
        check_vma=False,
    )
```

```python
import functools

import jax
import jax.numpy as jnp
from jax import lax
from jax.experimental import pallas as pl
from jax.experimental.pallas import tpu as pltpu
from jax.sharding import PartitionSpec as P

D = 8192
HD = 128
GROUP = 8
BLOCK = 256
DECODE_ROWS = 64
MASKED = -1e30
LOG2E = 1.4426950408889634
SCALE2 = HD ** (-0.5) * LOG2E
MIB = 1024 * 1024

bf16 = jnp.bfloat16
f32 = jnp.float32


def scores_of(rows, keys):
    return lax.dot_general(rows, keys, (((1,), (1,)), ((), ())), preferred_element_type=f32)


def place():
    index = lax.axis_index("ctx")
    return index // 4, index % 4, index // 4 % 2


def fill_values(aug_ref, index, block):
    aug_ref[index, :, :HD] = block[:, HD:]
    aug_ref[index, :, HD:] = jnp.ones((BLOCK, HD), bf16)


def weigh(parts, highest, aug_blocks):
    out = None
    for part, aug in zip(parts, aug_blocks):
        weights = jnp.exp2((part - highest) * SCALE2).astype(bf16)
        term = jnp.dot(weights, aug, preferred_element_type=f32)
        out = term if out is None else out + term
    return out


def max_of(parts):
    top = parts[0]
    for part in parts[1:]:
        top = jnp.maximum(top, part)
    return jnp.max(top, axis=-1, keepdims=True)


def in_turn(steps):
    parts = steps[0][0]()
    for i, (_, finish) in enumerate(steps):
        following = steps[i + 1][0]() if i + 1 < len(steps) else None
        finish(parts)
        parts = following


def flatten(target_ref, source_ref):
    for s in range(16):
        target_ref[s * 4 : s * 4 + 4] = source_ref[s]


def first_kernel(own_q, partner_q, hidden_in, rows_in, *refs):
    blocks = refs[:4]
    acc_ref, stat_ref, hidden_ref, rows_ref, aug_scr = refs[4:]
    flatten(hidden_ref, hidden_in)
    flatten(rows_ref, rows_in)
    _, row_y, parity = place()
    for group in range(2):
        for b in range(4):
            fill_values(aug_scr, group * 4 + b, blocks[b][group])
    lane = lax.broadcasted_iota(jnp.int32, (BLOCK, HD), 1)
    upper = lax.broadcasted_iota(jnp.int32, (BLOCK, BLOCK), 1) > lax.broadcasted_iota(
        jnp.int32, (BLOCK, BLOCK), 0
    )

    def shift_of(b):
        block_y = (row_y + (0, 3, 1, 2)[b]) % 4
        return jnp.where(block_y < row_y, 0.0, MASKED).astype(f32)

    def step(odd, h):
        side = 1 - parity if odd else parity
        at = pl.ds(pl.multiple_of(h * HD, HD), HD)

        def score():
            rows = jnp.where(side == 0, own_q[parity, :, at], partner_q[:, at])
            parts = []
            for b in range(4):
                part = scores_of(rows, blocks[b][side, :, :HD])
                if b == 0:
                    parts.append(jnp.where(upper, MASKED, part))
                else:
                    parts.append(part + shift_of(b))
            if odd:
                parts += [scores_of(rows, blocks[b][1 - side, :, :HD]) for b in range(4)]
            return parts

        def finish(parts):
            highest = max_of(parts)
            augs = [aug_scr[side * 4 + b] for b in range(4)]
            if odd:
                augs += [aug_scr[(1 - side) * 4 + b] for b in range(4)]
            mixed = weigh(parts, highest, augs)
            acc_ref[side, h] = mixed[:, :HD]
            old = jnp.where(lane == h, highest, stat_ref[side])
            stat_ref[side] = jnp.where(lane == h + 8, mixed[:, HD:], old)

        return score, finish

    for odd in (True, False):

        def four(half, carry, odd=odd):
            in_turn([step(odd, half * 4 + i) for i in range(4)])
            return carry

        lax.fori_loop(0, 2, four, 0)


def last_kernel(own, q_ref, acc_ref, stat_ref, *refs):
    kv_refs = refs[:4]
    out_ref, extra_ref, aug_scr, out_scr, sems = refs[-5:]
    extra_ref[...] = jnp.zeros_like(extra_ref)
    z, _, parity = place()
    side = 0 if own else 1
    if own:
        q_ref = q_ref.at[parity]
        out_ref = out_ref.at[parity]
    lane = lax.broadcasted_iota(jnp.int32, (BLOCK, HD), 1)

    def column(h):
        return jnp.sum(jnp.where(lane == h, stat_ref[side], 0.0), axis=-1, keepdims=True)

    def head_at(h):
        return pl.ds(pl.multiple_of(h * HD, HD), HD)

    def copy_of(half):
        at = pl.ds(pl.multiple_of(half * 4 * HD, 4 * HD), 4 * HD)
        return pltpu.make_async_copy(out_scr.at[:, at], out_ref.at[:, at], sems.at[half])

    @pl.when(z >= 2)
    def _():
        for b in range(8):
            fill_values(aug_scr, b, kv_refs[b // 2][b % 2])

        def step(h):
            def score():
                rows = q_ref[:, head_at(h)]
                return [scores_of(rows, kv_refs[b // 2][b % 2, :, :HD]) for b in range(8)]

            def finish(parts):
                before = column(h)
                highest = jnp.maximum(before, max_of(parts))
                mixed = weigh(parts, highest, [aug_scr[b] for b in range(8)])
                fade = jnp.exp2((before - highest) * SCALE2)
                total = column(h + 8) * fade + mixed[:, HD:]
                rows = (acc_ref[side, h] * fade + mixed[:, :HD]) / total
                out_scr[:, head_at(h)] = rows.astype(bf16)

            return score, finish

        def four(half, carry):
            in_turn([step(half * 4 + i) for i in range(4)])
            copy_of(half).start()
            return carry

        lax.fori_loop(0, 2, four, 0)

    @pl.when(z < 2)
    def _():
        def four(half, carry):
            for i in range(4):
                h = half * 4 + i
                out_scr[:, head_at(h)] = (acc_ref[side, h] / column(h + 8)).astype(bf16)
            copy_of(half).start()
            return carry

        lax.fori_loop(0, 2, four, 0)

    for half in range(2):
        copy_of(half).wait()


def segment_kernel(prompt_ref, _, rows0_ref, rows1_ref, *refs):
    kv_refs = refs[:8]
    out0_ref, out1_ref, pair_ref, aug_scr = refs[-4:]
    pair_ref[0] = refs[8][...]
    pair_ref[1] = refs[9][...]
    index, pool = lax.axis_index("ctx"), lax.axis_index("pd")
    parity = place()[2]

    def block_of(b, at):
        return kv_refs[b // 2][b % 2, :, at]

    for b in range(16):
        aug_scr[b, :, :HD] = block_of(b, slice(HD, 2 * HD))
        aug_scr[b, :, HD:] = jnp.ones((BLOCK, HD), bf16)
    lane = lax.broadcasted_iota(jnp.int32, (DECODE_ROWS, HD), 1)

    for which, rows_ref, out_ref in ((0, rows0_ref, out0_ref), (1, rows1_ref, out1_ref)):
        needed = prompt_ref[pool, index ^ (4 * which)] == parity

        @pl.when(needed)
        def _():
            stats = [jnp.zeros((DECODE_ROWS, HD), f32)]
            state = {}

            def step(tile, chunk):
                heads = range(tile * 4, tile * 4 + 4)
                blocks = range(chunk * 8, chunk * 8 + 8)

                def score():
                    rows = jnp.concatenate(
                        [rows_ref[:, h * HD : (h + 1) * HD] for h in heads], axis=0
                    )
                    return [scores_of(rows, block_of(b, slice(0, HD))) for b in blocks]

                def finish(parts):
                    top = max_of(parts)
                    augs = [aug_scr[b] for b in blocks]
                    if chunk == 0:
                        state[tile] = (top, weigh(parts, top, augs))
                        return
                    highest, mixed = state[tile]
                    top = jnp.maximum(top, highest)
                    mixed = mixed * jnp.exp2((highest - top) * SCALE2) + weigh(parts, top, augs)
                    total = mixed[:, HD:]
                    share = (mixed[:, :HD] / total).astype(bf16)
                    level = top * SCALE2 + jnp.log2(total)
                    for i, h in enumerate(heads):
                        at = slice(i * DECODE_ROWS, (i + 1) * DECODE_ROWS)
                        out_ref[:, h * HD : (h + 1) * HD] = share[at]
                        stats[0] = jnp.where(lane == h, level[at], stats[0])

                return score, finish

            in_turn([step(tile, chunk) for tile in range(2) for chunk in range(2)])
            stat = stats[0]
            high = stat.astype(bf16).astype(f32)
            middle = (stat - high).astype(bf16).astype(f32)
            low = stat - high - middle
            pieces = high + pltpu.roll(middle, 8, 1) + pltpu.roll(low, 16, 1)
            out_ref[:, GROUP * HD :] = pieces.astype(bf16)

        @pl.when(jnp.logical_not(needed))
        def _():
            out_ref[...] = jnp.zeros_like(out_ref)


def local_kernel(
    len_ref, _, cos_ref, sin_ref, gain_ref, q_ref, own_ref, twin_ref, *refs
):
    pairs = refs[:3]
    weight_ref, cache_ref = refs[3:5]
    out_ref, level_ref = refs[-2:]
    width = own_ref.shape[1]
    core, x = lax.axis_index("tp") % 2, lax.axis_index("tp") // 2
    ones = jnp.ones((BLOCK, HD), bf16)
    row = lax.broadcasted_iota(jnp.int32, (128, BLOCK), 0)
    slot = lax.broadcasted_iota(jnp.int32, (128, BLOCK), 1)
    fresh_row = lax.broadcasted_iota(jnp.int32, (128, DECODE_ROWS), 0) % 16
    fresh_slot = lax.broadcasted_iota(jnp.int32, (128, DECODE_ROWS), 1)

    groups = []
    for g in range(4):
        rows = jnp.concatenate(
            [q_ref[g * 16 : g * 16 + 16, h * HD : (h + 1) * HD] for h in range(GROUP)], axis=0
        )
        parts = []
        for j in range(4):
            s = g * 4 + j
            allowed = (row % 16 // 4 == j) & (slot < len_ref[s])
            parts.append(jnp.where(allowed, scores_of(rows, cache_ref[s, :, :HD]), MASKED))
        groups.append((rows, parts))

    squares = jnp.zeros((DECODE_ROWS, 1), f32)
    projected = jnp.zeros((DECODE_ROWS, 2 * HD), f32)
    for i, step in enumerate((0, 3, 1, 2)):
        for side in range(2):
            owner = ((x + step) % 4) * 2 + (core if side == 0 else 1 - core)
            if i == 0:
                wide = (own_ref, twin_ref)[side][...].astype(f32)
            else:
                wide = pairs[i - 1][side].astype(f32)
            at = pl.ds(pl.multiple_of(owner * width, width), width)
            squares = squares + jnp.sum(wide * wide, axis=-1, keepdims=True)
            scaled = (wide * gain_ref[:, at]).astype(bf16)
            projected = projected + jnp.dot(
                scaled, weight_ref[at], preferred_element_type=f32
            )
    normed = projected * lax.rsqrt(squares / D + 1e-6)
    key_rows = normed[:, :HD]
    turned = pltpu.roll(key_rows, HD // 2, 1)
    fresh_k = (key_rows * cos_ref[...] + turned * sin_ref[...]).astype(bf16)
    fresh_v = normed[:, HD:].astype(bf16)
    fresh_aug = jnp.concatenate([fresh_v, jnp.ones((DECODE_ROWS, HD), bf16)], axis=1)

    for g, (rows, parts) in enumerate(groups):
        at = slice(g * 16, (g + 1) * 16)
        augs = [
            jnp.concatenate([cache_ref[g * 4 + j, :, HD:], ones], axis=1) for j in range(4)
        ]
        behind = fresh_row + g * 16 - fresh_slot
        allowed = (behind >= 0) & (behind <= fresh_row % 4)
        fresh_part = jnp.where(allowed, scores_of(rows, fresh_k), MASKED)
        highest = jnp.maximum(max_of(parts), jnp.max(fresh_part, axis=-1, keepdims=True))
        mixed = weigh(parts + [fresh_part], highest, augs + [fresh_aug])
        total = mixed[:, HD:]
        share = mixed[:, :HD] / total
        level = highest * SCALE2 + jnp.log2(total)
        for h in range(GROUP):
            out_ref[at, h * HD : (h + 1) * HD] = share[h * 16 : (h + 1) * 16]
            level_ref[at, h * HD : (h + 1) * HD] = level[h * 16 : (h + 1) * 16]


def merge_kernel(
    prompt_ref, local_ref, level_ref, same_ref, other_ref, returned_ref, own_out, out_ref, full_ref,
    sem,
):
    del own_out
    parity = place()[2]
    copy = pltpu.make_async_copy(returned_ref, full_ref.at[1 - parity], sem)
    copy.start()
    lane = lax.broadcasted_iota(jnp.int32, (DECODE_ROWS, HD), 1)
    held_here = prompt_ref[1 - lax.axis_index("pd"), lax.axis_index("ctx")] == parity

    def merge(part_ref):
        pieces = part_ref[:, GROUP * HD :].astype(f32)
        for h in range(GROUP):
            at = slice(h * HD, (h + 1) * HD)
            mine = (lane == h) | (lane == h + 8) | (lane == h + 16)
            far = jnp.sum(jnp.where(mine, pieces, 0.0), axis=-1, keepdims=True)
            near = level_ref[:, at]
            top = jnp.maximum(far, near)
            far_share = jnp.exp2(far - top)
            near_share = jnp.exp2(near - top)
            mixed = part_ref[:, at].astype(f32) * far_share + local_ref[:, at] * near_share
            merged = mixed / (far_share + near_share)
            for s in range(16):
                out_ref[s, :, at] = merged[s * 4 : s * 4 + 4].astype(bf16)

    @pl.when(held_here)
    def _():
        merge(same_ref)

    @pl.when(jnp.logical_not(held_here))
    def _():
        merge(other_ref)

    copy.wait()


SMEM = pl.BlockSpec(memory_space=pltpu.SMEM)
VMEM = pl.BlockSpec(memory_space=pltpu.VMEM)
ANY = pl.BlockSpec(memory_space=pl.ANY)


def call(
    kernel, out_shape, args, scalars=0, scratch=(), flops=0, touched=0, exps=0, specs=None,
    out_specs=None, aliases=None, vmem=14,
):
    in_specs = [SMEM] * scalars + [VMEM] * (len(args) - scalars)
    for at, spec in (specs or {}).items():
        in_specs[at] = spec
    return pl.pallas_call(
        kernel,
        out_shape=out_shape,
        in_specs=in_specs,
        out_specs=out_specs or jax.tree.map(lambda _: VMEM, out_shape),
        scratch_shapes=list(scratch),
        input_output_aliases=aliases or {},
        compiler_params=pltpu.CompilerParams(vmem_limit_bytes=vmem * MIB),
        cost_estimate=pl.CostEstimate(flops=flops, bytes_accessed=touched, transcendentals=exps),
    )(*args)


def after(value, *others):
    return lax.optimization_barrier((value, *others))[0]


def y_turn(block, distance):
    route = [(i, i // 4 * 4 + (i % 4 + distance) % 4) for i in range(16)]
    return lax.ppermute(block, "ctx", route)


def z_swap(block, bits):
    return lax.ppermute(block, "ctx", [(i, i ^ (4 * bits)) for i in range(16)])


def y_all(block):
    return [block, y_turn(block, 1), y_turn(block, -1), y_turn(block, 2)]


def tp_turn(block, distance):
    return lax.ppermute(block, "tp", [(i, (i + distance) % 8) for i in range(8)])


def pool_swap(block, z_bits):
    route = [(i, (i ^ 1) ^ (8 * z_bits)) for i in range(32)]
    return lax.ppermute(block, ("ctx", "pd"), route)


def on_device(
    prefill_query,
    prefill_kv,
    decode_query,
    gen_cache,
    new_hidden,
    norm_gain,
    kv_weight,
    prompt_of,
    cached_len,
):
    queries = prefill_query[0]
    keyvals = prefill_kv[0]
    even = lax.axis_index("ctx") // 4 % 2 == 0
    shape = jax.ShapeDtypeStruct

    kv_keep = jnp.where(even, keyvals[0], keyvals[1])
    kv_give = jnp.where(even, keyvals[1], keyvals[0])
    from_z1 = z_swap(kv_give, 1)
    from_z2 = z_swap(kv_keep, 2)
    from_z3 = z_swap(kv_give, 3)
    q_give = lax.dynamic_index_in_dim(queries, even.astype(jnp.int32), 0, keepdims=False)
    samples, steps, width = new_hidden.shape[2:]
    decode_rows = samples * steps
    from_z1, q_give = lax.optimization_barrier((from_z1, q_give))
    first_pair, q_give = lax.optimization_barrier((jnp.stack([kv_keep, from_z1]), q_give))
    group01 = y_all(first_pair)
    q_partner = z_swap(q_give, 1)
    group23 = y_all(jnp.stack([from_z2, from_z3]))

    lengths = cached_len[0, 0]
    half = HD // 2
    frequency = 1000000.0 ** (-jnp.arange(half, dtype=f32) * 2.0 / HD)
    positions = (4096 + lengths[:, None] + jnp.arange(steps, dtype=jnp.int32)[None, :]).astype(f32)
    angles = positions.reshape(-1)[:, None] * frequency
    cosine, sine = jnp.cos(angles), jnp.sin(angles)
    cos_all = jnp.concatenate([cosine, cosine], axis=-1)
    sin_all = jnp.concatenate([-sine, sine], axis=-1)

    token = shape((8, HD), f32)
    flat = shape((decode_rows, width), bf16)
    acc, stat, hidden, step_rows = call(
        first_kernel,
        (shape((2, GROUP, BLOCK, HD), f32), shape((2, BLOCK, HD), f32), flat, flat),
        (queries, q_partner, new_hidden[0, 0], decode_query[0, 0], *group01),
        scratch=(
            pltpu.VMEM((8, BLOCK, 2 * HD), bf16),
        ),
        flops=3 * 2048 * 1024 * 512,
        touched=4 << 20,
        exps=3 * 2048 * 1024,
    )
    twin = lax.ppermute(hidden, "tp", [(i, i ^ 1) for i in range(8)])
    rows_pair = [pool_swap(step_rows, 0), pool_swap(step_rows, 1)]

    def finish(own, q_rows, extra):
        out_rows = (BLOCK, GROUP * HD)
        return call(
            functools.partial(last_kernel, own),
            (shape((2, *out_rows) if own else out_rows, bf16), token),
            (q_rows, acc, stat, *group23, *extra),
            scratch=(
                pltpu.VMEM((8, BLOCK, 2 * HD), bf16),
                pltpu.VMEM(out_rows, bf16),
                pltpu.SemaphoreType.DMA((2,)),
            ),
            specs={7: ANY} if own else None,
            out_specs=(ANY, VMEM),
            flops=2 * 2048 * 1024 * 512,
            touched=4 << 20,
            exps=2 * 2048 * 1024,
        )

    out_partner, partner_done = finish(False, q_partner, ())
    returned = z_swap(out_partner, 1)
    part = shape((decode_rows, width + HD), bf16)
    segment0, segment1, pair = call(
        segment_kernel,
        (part, part, shape((2, decode_rows, width), bf16)),
        (prompt_of, partner_done, *rows_pair, *group01, *group23, hidden, twin),
        specs={1: ANY},
        scalars=1,
        scratch=(pltpu.VMEM((16, BLOCK, 2 * HD), bf16),),
        flops=1024 * 4096 * 512,
        touched=3 << 20,
        exps=1024 * 4096,
    )
    back0 = pool_swap(segment0, 0)
    back1 = pool_swap(segment1, 1)
    pairs = [tp_turn(pair, 2), tp_turn(pair, -2), tp_turn(pair, 4)]
    out_own, own_done = finish(True, queries, (pair,))
    local_out, local_level = call(
        local_kernel,
        (shape((decode_rows, width), f32), shape((decode_rows, width), f32)),
        (
            lengths,
            own_done,
            cos_all,
            sin_all,
            norm_gain[None],
            step_rows,
            hidden,
            twin,
            *pairs,
            kv_weight,
            gen_cache[0, 0],
        ),
        scalars=1,
        specs={1: ANY},
        flops=2 * 64 * D * 256,
        touched=8 << 20,
        exps=512 * 320,
    )

    merged, segment_out = call(
        merge_kernel,
        (shape((samples, steps, width), bf16), shape(queries.shape, bf16)),
        (prompt_of, local_out, local_level, back0, back1, returned, out_own),
        scalars=1,
        scratch=(pltpu.SemaphoreType.DMA,),
        flops=512 * HD * 8,
        touched=1 << 20,
        exps=512 * HD * 2,
        specs={5: ANY, 6: ANY},
        out_specs=(VMEM, ANY),
        aliases={6: 1},
        vmem=8,
    )
    return (segment_out[None], merged[None, None])


def solution(mesh):
    placed = (
        P("pd", None, "ctx", "tp"),
        P("pd", None, "ctx", "tp"),
        P("pd", "ctx", None, None, "tp"),
        P("pd", "ctx", None, None, "tp"),
        P("pd", "ctx", None, None, "tp"),
        P(),
        P(None, "tp"),
        P(),
        P("pd", "ctx", None),
    )
    return jax.shard_map(
        on_device,
        mesh=mesh,
        in_specs=placed,
        out_specs=(P("pd", None, "ctx", "tp"), P("pd", "ctx", None, None, "tp")),
        check_vma=False,
    )
```
